512 devices in a mesh: seq: 32 (over x, z_lo), expert: 8 (over z_hi, y), mp: 2 (over core).
Axes of the slice: x: 4, y: 4, z: 16 (z_hi: 2, z_lo: 8; z = z_hi * 8 + z_lo), core: 2. Of those that a mesh axis runs over, the one named last changes fastest.
Arguments:
- queries: bfloat16 [8, 32, 128, 4096], P('expert', 'seq', None, 'mp'), may hold values from -6 to 6
- out_grad: bfloat16 [8, 32, 128, 4096], P('expert', 'seq', None, 'mp'), may hold values from -6 to 6
- prompt_kv: bfloat16 [8, 1024, 2, 256], P('expert', 'seq', None, 'mp'), may hold values from -6 to 6
- resp_kv: bfloat16 [8, 32, 128, 2, 256], P('expert', 'seq', None, None, 'mp'), may hold values from -6 to 6
- lengths: int32 [8, 32], P('expert', 'seq'), may hold values from 1 to 128, 3072 in all within a row
- grads: bfloat16 [8, 32, 128, 2048], P('expert', 'seq'), may hold values from -6 to 6
- routes: int32 [8, 32, 128, 8], P('expert', 'seq'), may hold values from 0 to 127, all different within a row; in each aligned block of 128 rows (0 to 127, 128 to 255, ..., all dimensions but the last counted through in order) at most 16 rows name the same one
- gates: float32 [8, 32, 128, 8], P('expert', 'seq'), may hold values from 0.1 to 1
- down_weight: bfloat16 [8, 1536, 2048], P('expert', 'mp'), may hold values from -0.125 to 0.125
Outputs:
- prompt_dkv: float32 [8, 1024, 2, 256], P('expert', 'seq', None, 'mp')
- resp_dkv: float32 [8, 32, 128, 2, 256], P('expert', 'seq', None, None, 'mp')
- expert_grad: bfloat16 [32, 8, 8, 16, 1536], P('seq', None, 'expert', None, 'mp')
The draws below stay inside these ranges and needn't reach their ends.
Inputs may be any that keep to these rules, and one draw needn't show every extreme that they name: `routes`: the 8 experts of a token differ; among the rows of one device no expert is named by more than 16 rows.
All inputs are finite; a program needn't handle non-finite values. No bound on the sum of `lengths` on one device may be relied on, other than what follows from the above.
Results may differ from the reference program's by a relative error of at most 0.0049.
Values may be sent and summed in bfloat16 or wider, within the bound.
A program may use at most 64 MiB of HBM per device.

```python
import math
import jax
import jax.numpy as jnp
import numpy as np
from jax import lax

D = 2048
FF = 1536
QH = 32
KVH = 2
HD = 128
EXPERTS_ALL = 128
TOP = 8
LEN = 128
GROUPS = 8
RESP = 32
PROMPT = 1024
EXPERTS = 8
CAP = 16


def draw_queries(key, part):
    key = jax.random.fold_in(key, 1)
    full_shape = (GROUPS, RESP, LEN, QH * HD)
    values_base = jnp.clip(jax.random.normal(key, full_shape, jnp.float32), -6.0, 6.0)
    return values_base.astype(jnp.bfloat16)


def draw_prompt_kv(key, part):
    key = jax.random.fold_in(key, 2)
    full_shape = (GROUPS, PROMPT, 2, KVH * HD)
    values_base = jnp.clip(jax.random.normal(key, full_shape, jnp.float32), -6.0, 6.0)
    return values_base.astype(jnp.bfloat16)


def levels(rng, dims, cuts, smallest, high):
    gain, own = 1.0, jax.random.fold_in(rng, 6)
    for axis_at, blocks in cuts:
        steps = jnp.exp(jax.random.uniform(jax.random.fold_in(own, axis_at), (blocks,), jnp.float32, smallest / len(cuts), high / len(cuts)))
        gain = gain * jnp.repeat(steps, dims[axis_at] // blocks).reshape([-1 if axis == axis_at else 1 for axis in range(len(dims))])
    return gain


def split_up(amount, total, reach, lean):
    portions = [(1 << 20) // math.isqrt(standing ** lean) + 1 for standing in range(2, amount + 1)]
    surplus, holding = total - reach - (amount - 1), [1] * (amount - 1)
    while surplus > 0:
        movable = [i for i in range(amount - 1) if holding[i] < reach]
        pool, budget = sum([portions[i] for i in movable]), surplus
        for i in movable:
            extra = min(reach - holding[i], max(1, budget * portions[i] // pool), surplus)
            holding[i] = holding[i] + extra
            surplus = surplus - extra
    return np.array([reach] + holding)


def uneven(rng, amount, total, limit, skew):
    if amount == 2:
        one = jax.random.randint(rng, (), max(1, total - limit), min(limit, total - 1) + 1)
        return jnp.stack([one, total - one])
    sizes = jnp.asarray(split_up(amount, total, limit, skew), jnp.int32)
    twos = (amount - 1) // 2
    donor, taker = sizes[1:1 + 2 * twos:2], sizes[2:2 + 2 * twos:2]
    room = jnp.minimum(donor - 1, limit - taker)
    shifted = jax.random.randint(jax.random.fold_in(rng, 1), (twos,), 0, 1 << 20) % (room + 1)
    sizes = sizes.at[1:1 + 2 * twos:2].set(donor - shifted).at[2:2 + 2 * twos:2].set(taker + shifted)
    return sizes[jax.random.permutation(jax.random.fold_in(rng, 2), amount)]


def assign_block(stream_key, own, number, rows, number_of, top, bound, slope):
    order = jax.random.permutation(stream_key, number_of)
    crowded, common = portions_of(number_of, rows * top, bound, slope, True), portions_of(number_of, rows * top, bound, slope, False)
    places = jnp.arange(number_of)

    def named(tallies, offset_by):
        used = int((tallies > 0).sum())
        fixed = max(1, used // 4)
        passed = fixed + (places - fixed + offset_by * (used - fixed)) % max(1, number_of - fixed)
        return jnp.zeros((number_of,), jnp.int32).at[order[jnp.where(places < fixed, places, passed)]].set(jnp.asarray(tallies, jnp.int32))

    tallies = jnp.where(number % 4 == 0, named(crowded, number // 4), named(common, number - number // 4 - 1))
    mixed = jax.random.permutation(jax.random.fold_in(own, 3), number_of)
    giver, receiver = mixed[0:number_of // 2 * 2:2], mixed[1:number_of // 2 * 2:2]
    margin = jnp.minimum(tallies[giver] - 1, bound - tallies[receiver]) // 2
    margin = jnp.where((giver == order[0]) | (receiver == order[0]) | (tallies[receiver] == 0), 0, jnp.maximum(margin, 0))
    passed = jax.random.randint(jax.random.fold_in(own, 4), (number_of // 2,), 0, 1 << 20) % (margin + 1)
    tallies = tallies.at[giver].add(-passed).at[receiver].add(passed)
    labels = jnp.searchsorted(jnp.cumsum(tallies), jnp.arange(rows * top), side="right").astype(jnp.int32)
    listing = labels.reshape(top, rows).T
    listing = listing[jax.random.permutation(jax.random.fold_in(own, 1), rows)]
    offset_by = jax.random.randint(jax.random.fold_in(own, 2), (rows, 1), 0, top)
    return jnp.take_along_axis(listing, (jnp.arange(top)[None, :] + offset_by) % top, axis=1)


def portions_of(count, total, limit, lean, full):
    loads = [(1 << 20) // math.isqrt(standing ** lean) + 1 for standing in range(1, count + 1)]
    largest = limit if full else min(limit, max(-(-total // count), total * loads[0] // sum(loads)))
    least = 1 if total - largest >= count - 1 else 0
    given, spare = [largest] + [least] * (count - 1), total - largest - least * (count - 1)
    while spare > 0:
        free = [i for i in range(1, count) if given[i] < largest] or [i for i in range(1, count) if given[i] < limit]
        pool, budget = sum([loads[i] for i in free]), spare
        for i in free:
            addition = min(limit - given[i], max(1, budget * loads[i] // pool), spare)
            given[i] = given[i] + addition
            spare = spare - addition
    return np.array(given)


def noise(own_key, shape, deviation, bound, cuts=(), dtype=jnp.bfloat16):
    factor_of = levels(own_key, shape, cuts, -0.22, 0.18) if cuts else 1.0
    values = jax.random.normal(own_key, shape, jnp.float32) * deviation * factor_of
    return jnp.minimum(jnp.maximum(values, -bound), bound).astype(dtype)


def setup_inputs(seed: int = 0) -> dict:
    arg_keys = jax.random.split(jax.random.key(seed), 10)
    queries = draw_queries(jax.random.fold_in(arg_keys[9], 71), 0)
    out_grad = noise(arg_keys[1], (GROUPS, RESP, LEN, QH * HD), 1.0, 6.0, ((0, 8), (1, 32), (3, 2)))
    prompt_kv = draw_prompt_kv(jax.random.fold_in(arg_keys[9], 71), 0)
    resp_kv = noise(arg_keys[3], (GROUPS, RESP, LEN, 2, KVH * HD), 1.0, 6.0, ((0, 8), (1, 32), (4, 2)))
    lengths = jax.vmap(lambda own: uneven(own, RESP, (3 * LEN * RESP) // 4, LEN, 2))(jax.random.split(arg_keys[4], GROUPS)).reshape((GROUPS, RESP)).astype(jnp.int32)
    grads = noise(arg_keys[5], (GROUPS, RESP, LEN, D), 1.0, 6.0, ((0, 8), (1, 32)))
    routes_keys = jax.random.split(jax.random.fold_in(arg_keys[6], 1), GROUPS * RESP * LEN // LEN)
    routes_turns = jax.random.permutation(jax.random.fold_in(arg_keys[6], 3), GROUPS * RESP * LEN // LEN)
    routes = jax.vmap(lambda own, number: assign_block(jax.random.fold_in(arg_keys[6], 2), own, number, LEN, EXPERTS_ALL, TOP, LEN // 8, 2))(routes_keys, routes_turns).reshape((GROUPS, RESP, LEN, TOP))
    gates = jnp.clip(jnp.exp(math.log(1.0) - 2.3025851 * jax.random.uniform(arg_keys[7], (GROUPS, RESP, LEN, TOP), jnp.float32) ** levels(arg_keys[7], (GROUPS, RESP, LEN, TOP), ((0, 8), (1, 32)), -0.2, 0.2)), 0.1, 1.0)
    down_weight = noise(arg_keys[8], (EXPERTS, FF, D), D ** -0.5, 0.125, ((0, 8), (1, 2)))
    return {"queries": queries, "out_grad": out_grad, "prompt_kv": prompt_kv, "resp_kv": resp_kv, "lengths": lengths, "grads": grads, "routes": routes, "gates": gates, "down_weight": down_weight}


def attend(query_rows, grad_out, prompt_keys, prompt_values, own_keys, own_values, length):
    row_count = query_rows.shape[0]
    group_size = QH // KVH
    score_scale = HD ** -0.5
    query_heads = query_rows.astype(jnp.float32).reshape(row_count, KVH, group_size, HD)
    key_rows = jnp.concatenate([prompt_keys, own_keys], 0).astype(jnp.float32).reshape(-1, KVH, HD)
    value_rows = jnp.concatenate([prompt_values, own_values], 0).astype(jnp.float32).reshape(-1, KVH, HD)
    key_total = key_rows.shape[0]
    position = jnp.arange(row_count)
    allowed = jnp.concatenate([jnp.ones((row_count, prompt_keys.shape[0]), jnp.bool_), position[None, :] <= position[:, None]], 1)
    scores = jnp.einsum('icgd,jcd->cgij', query_heads, key_rows) * score_scale
    scores = jnp.where(allowed, scores, -jnp.inf)
    numerators = jnp.exp(scores - jnp.max(scores, -1, keepdims=True))
    attention = numerators / jnp.sum(numerators, -1, keepdims=True)
    attention_low = lax.optimization_barrier(attention.astype(jnp.bfloat16)).astype(jnp.float32)
    grad_rows = jnp.where((position < length)[:, None], grad_out, jnp.zeros_like(grad_out))
    grad_heads = grad_rows.astype(jnp.float32).reshape(row_count, KVH, group_size, HD)
    grad_probs = jnp.einsum('icgd,jcd->cgij', grad_heads, value_rows)
    row_delta = jnp.sum(attention * grad_probs, -1, keepdims=True)
    grad_scores = attention * (grad_probs - row_delta) * score_scale
    grad_low = lax.optimization_barrier(grad_scores.astype(jnp.bfloat16)).astype(jnp.float32)
    grad_keys = jnp.einsum('cgij,icgd->jcd', grad_low, query_heads)
    grad_values = jnp.einsum('cgij,icgd->jcd', attention_low, grad_heads)
    return jnp.stack([grad_keys.reshape(key_total, KVH * HD), grad_values.reshape(key_total, KVH * HD)], 1)


def dispatch_rows(token_rows, route_ids, gate_rows, length):
    row_count = token_rows.shape[0]
    expert_ids = jnp.arange(EXPERTS).astype(jnp.int32)
    matches = route_ids[:, :, None] == expert_ids[None, None, :]
    named_rows = jnp.any(matches, 1)
    valid_rows = (jnp.arange(row_count) < length).astype(jnp.float32)
    route_weight = jnp.sum(jnp.where(matches, gate_rows[:, :, None], jnp.zeros_like(gate_rows[:, :, None])), 1) * valid_rows[:, None]
    slot_index = jnp.cumsum(named_rows.astype(jnp.int32), 0) - 1
    selection = named_rows[:, :, None] & (slot_index[:, :, None] == jnp.arange(CAP).astype(jnp.int32)[None, None, :])
    picked = jnp.einsum('ixc,id->xcd', selection.astype(jnp.float32), token_rows.astype(jnp.float32), precision=lax.Precision.HIGHEST)
    slot_gate = jnp.einsum('ixc,ix->xc', selection.astype(jnp.float32), route_weight, precision=lax.Precision.HIGHEST)
    return (picked * slot_gate[:, :, None]).astype(jnp.bfloat16)


def reference(queries, out_grad, prompt_kv, resp_kv, lengths, grads, routes, gates, down_weight):
    prompt_parts = []
    own_parts = []
    for group_idx in range(GROUPS):
        prompt_keys = prompt_kv[group_idx, :, 0]
        prompt_values = prompt_kv[group_idx, :, 1]

        def respond(inputs, prompt_keys=prompt_keys, prompt_values=prompt_values):
            return attend(inputs[0], inputs[1], prompt_keys, prompt_values, inputs[2], inputs[3], inputs[4])

        terms = lax.map(respond, (queries[group_idx], out_grad[group_idx], resp_kv[group_idx, :, :, 0], resp_kv[group_idx, :, :, 1], lengths[group_idx]))
        prompt_parts.append(jnp.sum(terms[:, :PROMPT], 0))
        own_parts.append(terms[:, PROMPT:])
    prompt_dkv = jnp.stack(prompt_parts, 0)
    resp_dkv = jnp.stack(own_parts, 0)
    weight_wide = down_weight.astype(jnp.float32)

    def expert_rows(inputs):
        selected = dispatch_rows(inputs[0], inputs[1], inputs[2], inputs[3])
        return jnp.einsum('xcd,xfd->xcf', selected.astype(jnp.float32), weight_wide, precision=lax.Precision.HIGHEST).astype(jnp.bfloat16)

    flat_out = lax.map(expert_rows, (grads.reshape(GROUPS * RESP, LEN, D), routes.reshape(GROUPS * RESP, LEN, TOP), gates.reshape(GROUPS * RESP, LEN, TOP), lengths.reshape(GROUPS * RESP)))
    expert_grad = jnp.transpose(flat_out.reshape(GROUPS, RESP, EXPERTS, CAP, FF), (1, 0, 2, 3, 4))
    return (prompt_dkv, resp_dkv, expert_grad)
```

```python
import functools
import math

import jax
import jax.numpy as jnp
from jax import lax
from jax.experimental import pallas as pl
from jax.experimental.pallas import tpu as pltpu
from jax.sharding import PartitionSpec as P

HD = 128
SCALE = HD**-0.5
SCALE2 = SCALE * math.log2(math.e)
MESH = pl.DeviceIdType.MESH
F32 = jnp.float32
BF16 = jnp.bfloat16
NT = (((1,), (1,)), ((), ()))
NN = (((1,), (0,)), ((), ()))
TILE = 512


def kernel(
    nx,
    nz,
    len_ref,
    pkv_ref,
    rkv_ref,
    routes_ref,
    gates_ref,
    q_hbm,
    g_hbm,
    tok_hbm,
    w_hbm,
    pout,
    rout,
    eout,
    q,
    g,
    tok,
    w,
    gath,
    num,
    prob,
    stat,
    low_a,
    low_g,
    part1,
    recv1,
    own_sum,
    part2,
    recv2,
    rows_out,
    rows_in,
    local_sem,
    zs,
    zr,
    xs,
    xr,
    es,
    er,
    cs,
    cr,
    s1,
    r1,
    s2,
    r2,
):
    seq = lax.axis_index("seq")
    me_e = lax.axis_index("expert")
    me_c = lax.axis_index("mp")
    me_x, me_z = seq // nz, seq % nz
    ne = rows_out.shape[0]
    cap = rows_out.shape[1]
    half = rows_out.shape[2]
    rows_all = q.shape[0]
    heads = rows_all // 128
    toks = gath.shape[3]
    blk = nz * toks

    def at_x(o):
        return {"seq": (me_x + o) % nx * nz + me_z}

    def at_z(o):
        return {"seq": me_x * nz + (me_z + o) % nz}

    def at_e(o):
        return {"expert": (me_e + o) % ne}

    sibling = {"mp": 1 - me_c}

    barrier = pltpu.get_barrier_semaphore()
    peers = [at_x(o) for o in range(1, nx)] + [at_z(o) for o in range(1, nz)]
    peers += [at_e(o) for o in range(1, ne)] + [sibling]
    for peer in peers:
        pl.semaphore_signal(barrier, inc=1, device_id=peer, device_id_type=MESH)

    tok_copy = pltpu.make_async_copy(
        tok_hbm.at[:, pl.ds(pl.multiple_of(me_c * half, half), half)], tok, local_sem.at[2]
    )
    tok_copy.start()
    for h in range(heads):
        cols = slice(h * HD, (h + 1) * HD)
        pltpu.make_async_copy(q_hbm.at[:, cols], q.at[h * 128 : (h + 1) * 128], local_sem.at[0]).start()
        pltpu.make_async_copy(g_hbm.at[:, cols], g.at[h * 128 : (h + 1) * 128], local_sem.at[1]).start()
    w_copy = pltpu.make_async_copy(w_hbm, w, local_sem.at[3])
    w_copy.start()
    gath[me_x, me_z] = pkv_ref[...]
    pl.semaphore_wait(barrier, len(peers))

    sends = []

    def remote(src, dst, send_sem, recv_sem, peer):
        copy = pltpu.make_async_remote_copy(
            src_ref=src,
            dst_ref=dst,
            send_sem=send_sem,
            recv_sem=recv_sem,
            device_id=peer,
            device_id_type=MESH,
        )
        copy.start()
        sends.append(copy)

    z_order = sorted(range(1, nz), key=lambda o: min(o, nz - o))
    own_block = gath.at[me_x, me_z]
    for o in reversed(z_order):
        remote(own_block, own_block, zs.at[o - 1], zr.at[me_z], at_z(o))

    def forward(k, zb):
        block = gath.at[me_x, zb]
        for o in range(1, nx):
            remote(block, block, xs.at[o - 1, k], xr.at[o - 1], at_x(o))

    forward(0, me_z)

    length = len_ref[0]
    lane = lax.broadcasted_iota(jnp.int32, (1, 128), 1)
    route_t = routes_ref[...].astype(F32).T
    gate_t = gates_ref[...].T
    valid = (lane < length).astype(F32)
    named, weight = [], []
    for e in range(ne):
        hit = route_t == float(e)
        named.append(jnp.max(hit.astype(F32), 0, keepdims=True))
        weight.append(jnp.sum(jnp.where(hit, gate_t, 0.0), 0, keepdims=True) * valid)
    named_all = jnp.concatenate(named, 0)
    upper = (
        lax.broadcasted_iota(jnp.int32, (128, 128), 0) <= lax.broadcasted_iota(jnp.int32, (128, 128), 1)
    ).astype(BF16)
    slot = lax.dot_general(named_all.astype(BF16), upper, NN, preferred_element_type=F32) - 1.0
    slot_id = lax.broadcasted_iota(jnp.int32, (cap, 128), 0).astype(F32)
    select, slot_gate = [], []
    for e in range(ne):
        chosen = jnp.where(slot[e : e + 1] == slot_id, named[e], 0.0)
        select.append(chosen)
        slot_gate.append(jnp.sum(chosen * weight[e], 1, keepdims=True))
    select = jnp.concatenate(select, 0).astype(BF16)
    slot_gate = jnp.concatenate(slot_gate, 0)
    tok_copy.wait()
    picked = lax.dot_general(select, tok[...], NN, preferred_element_type=F32)
    rows_out[...] = (picked * slot_gate).astype(BF16).reshape(ne, cap, half)

    for k, o in enumerate(z_order):
        zb = (me_z + o) % nz
        block = gath.at[me_x, zb]
        pltpu.make_async_copy(block, block, zr.at[zb]).wait()
        forward(k + 1, zb)

    for o in range(1, ne):
        there = (me_e + o) % ne
        remote(rows_out.at[there], rows_in.at[me_c, me_e], es.at[o - 1], er.at[me_e], at_e(o))
    rows_in[me_c, me_e] = rows_out[me_e]

    pltpu.make_async_copy(q, q, local_sem.at[0]).wait()
    pltpu.make_async_copy(g, g, local_sem.at[1]).wait()
    row_at = lax.broadcasted_iota(jnp.int32, (128, HD), 0)
    for h in range(heads):
        part = g[h * 128 : (h + 1) * 128, :]
        g[h * 128 : (h + 1) * 128, :] = jnp.where(row_at < length, part.astype(F32), 0.0).astype(BF16)

    def forward_block(b, keys, values, causal):
        n = keys.shape[0]
        for t in range(rows_all // TILE):
            rows = slice(t * TILE, (t + 1) * TILE)
            score = lax.dot_general(keys, q[rows, :], NT, preferred_element_type=F32)
            if causal:
                key_at = lax.broadcasted_iota(jnp.int32, (n, TILE), 0)
                query_at = lax.broadcasted_iota(jnp.int32, (n, TILE), 1) % 128
                score = jnp.where(key_at <= query_at, score, -jnp.inf)
            top = jnp.max(score, 0, keepdims=True)
            exps = jnp.exp2((score - top) * SCALE2)
            probs = lax.dot_general(values, g[rows, :], NT, preferred_element_type=F32)
            stat[0, b : b + 1, rows] = top
            stat[1, b : b + 1, rows] = jnp.sum(exps, 0, keepdims=True)
            stat[2, b : b + 1, rows] = jnp.sum(exps * probs, 0, keepdims=True)
            num[b, 0:n, rows] = exps
            prob[b, 0:n, rows] = probs

    own_b = nx
    forward_block(own_b, rkv_ref[0], rkv_ref[1], True)
    x_order = sorted(range(1, nx), key=lambda o: min(o, nx - o))
    for b, o in enumerate([0] + x_order):
        xb = (me_x + nx - o) % nx
        if o:
            came = gath.at[xb]
            pltpu.make_async_copy(came, came, xr.at[o - 1]).wait()
        forward_block(
            b, gath[xb, :, 0].reshape(blk, HD), gath[xb, :, 1].reshape(blk, HD), False
        )

    nb = nx + 1
    top = stat[0, 0:nb, :]
    factor = jnp.exp2((top - jnp.max(top, 0, keepdims=True)) * SCALE2)
    inverse = 1.0 / jnp.sum(stat[1, 0:nb, :] * factor, 0, keepdims=True)
    delta = jnp.sum(stat[2, 0:nb, :] * factor, 0, keepdims=True) * inverse
    stat[0, 0:nb, :] = factor * inverse
    stat[1, 0:1, :] = delta

    def backward_block(b, part, n):
        keys = slice(part * n, (part + 1) * n)
        for t in range(rows_all // 256):
            rows = slice(t * 256, (t + 1) * 256)
            attention = num[b, keys, rows] * stat[0, b : b + 1, rows]
            grad = attention * ((prob[b, keys, rows] - stat[1, 0:1, rows]) * SCALE)
            low_a[part, 0:n, rows] = attention.astype(BF16)
            low_g[part, 0:n, rows] = grad.astype(BF16)
        grad_v = lax.dot_general(low_a[part, 0:n, :], g[...], NN, preferred_element_type=F32)
        grad_k = lax.dot_general(low_g[part, 0:n, :], q[...], NN, preferred_element_type=F32)
        return grad_k, grad_v

    sub = min(128, blk)
    for b, o in reversed(list(enumerate([0] + x_order))):
        for part in range(blk // sub):
            grad_k, grad_v = backward_block(b, part, sub)
            keys = slice(part * sub, (part + 1) * sub)
            if o:
                part1[b - 1, 0, keys, :] = grad_k.astype(BF16)
                part1[b - 1, 1, keys, :] = grad_v.astype(BF16)
            else:
                own_sum[0, keys, :] = grad_k
                own_sum[1, keys, :] = grad_v
        if o:
            back = nx - o
            remote(part1.at[b - 1], recv1.at[o - 1], s1.at[o - 1], r1.at[o - 1], at_x(back))

    for o in range(1, nx):
        pltpu.make_async_copy(recv1.at[o - 1], recv1.at[o - 1], r1.at[o - 1]).wait()
    for zb in range(nz):
        keys = slice(zb * toks, (zb + 1) * toks)
        for kv in range(2):
            total = own_sum[kv, keys, :]
            for o in range(1, nx):
                total = total + recv1[o - 1, kv, keys, :].astype(F32)
            own_sum[kv, keys, :] = total
            part2[zb, kv] = total.astype(BF16)
    for o in reversed(z_order):
        zb = (me_z + o) % nz
        remote(part2.at[zb], recv2.at[me_z], s2.at[o - 1], r2.at[me_z], at_z(o))

    for o in range(1, ne):
        there = (me_e + o) % ne
        came = rows_in.at[me_c, there]
        pltpu.make_async_copy(came, came, er.at[there]).wait()
    remote(rows_in.at[me_c], rows_in.at[me_c], cs.at[0], cr.at[0], sibling)

    grad_k, grad_v = backward_block(own_b, 0, 128)
    rout[0] = grad_k
    rout[1] = grad_v

    w_copy.wait()
    other = rows_in.at[1 - me_c]
    pltpu.make_async_copy(other, other, cr.at[0]).wait()
    hidden = lax.dot_general(
        rows_in[0].reshape(ne * cap, half), w[:, 0:half], NT, preferred_element_type=F32
    )
    hidden = hidden + lax.dot_general(
        rows_in[1].reshape(ne * cap, half), w[:, half : 2 * half], NT, preferred_element_type=F32
    )
    eout[...] = hidden.astype(BF16).reshape(eout.shape)

    mine = pl.ds(pl.multiple_of(me_z * toks, toks), toks)
    total_k, total_v = own_sum[0, mine, :], own_sum[1, mine, :]
    for o in z_order:
        zb = (me_z + o) % nz
        came = recv2.at[zb]
        pltpu.make_async_copy(came, came, r2.at[zb]).wait()
        total_k = total_k + recv2[zb, 0].astype(F32)
        total_v = total_v + recv2[zb, 1].astype(F32)
    pout[0] = total_k
    pout[1] = total_v
    for copy in sends:
        copy.wait_send()


def local(nx, queries, out_grad, prompt_kv, resp_kv, lengths, grads, routes, gates, down_weight):
    ne = lax.axis_size("expert")
    toks = prompt_kv.shape[1]
    rows = queries.shape[2]
    width = queries.shape[3]
    heads = width // HD
    nz = lax.axis_size("seq") // nx
    features = grads.shape[3]
    half = features // 2
    hidden = down_weight.shape[1]
    cap = rows // 8
    blk = nz * toks
    vmem = pl.BlockSpec(memory_space=pltpu.VMEM)
    hbm = pl.BlockSpec(memory_space=pl.ANY)
    dma = pltpu.SemaphoreType.DMA
    out = pl.pallas_call(
        functools.partial(kernel, nx, nz),
        out_shape=[
            jax.ShapeDtypeStruct((2, toks, HD), F32),
            jax.ShapeDtypeStruct((2, rows, HD), F32),
            jax.ShapeDtypeStruct((ne, cap, hidden), BF16),
        ],
        in_specs=[pl.BlockSpec(memory_space=pltpu.SMEM)] + [vmem] * 4 + [hbm] * 4,
        out_specs=[vmem] * 3,
        scratch_shapes=[
            pltpu.VMEM((heads * rows, HD), BF16),
            pltpu.VMEM((heads * rows, HD), BF16),
            pltpu.VMEM((rows, half), BF16),
            pltpu.VMEM((hidden, features), BF16),
            pltpu.VMEM((nx, nz, 2, toks, HD), BF16),
            pltpu.VMEM((nx + 1, max(blk, rows), heads * rows), F32),
            pltpu.VMEM((nx + 1, max(blk, rows), heads * rows), F32),
            pltpu.VMEM((3, 8, heads * rows), F32),
            pltpu.VMEM((2, 128, heads * rows), BF16),
            pltpu.VMEM((2, 128, heads * rows), BF16),
            pltpu.VMEM((nx - 1, 2, blk, HD), BF16),
            pltpu.VMEM((nx - 1, 2, blk, HD), BF16),
            pltpu.VMEM((2, blk, HD), F32),
            pltpu.VMEM((nz, 2, toks, HD), BF16),
            pltpu.VMEM((nz, 2, toks, HD), BF16),
            pltpu.VMEM((ne, cap, half), BF16),
            pltpu.VMEM((2, ne, cap, half), BF16),
            dma((4,)),
            dma((nz - 1,)),
            dma((nz,)),
            dma((nx - 1, nz)),
            dma((nx - 1,)),
            dma((ne - 1,)),
            dma((ne,)),
            dma((1,)),
            dma((1,)),
            dma((nx - 1,)),
            dma((nx - 1,)),
            dma((nz - 1,)),
            dma((nz,)),
        ],
        compiler_params=pltpu.CompilerParams(
            collective_id=0, has_side_effects=True, vmem_limit_bytes=60 << 20
        ),
        name="moe_attention_backward",
    )(
        lengths[0],
        prompt_kv[0].transpose(1, 0, 2),
        resp_kv[0, 0].transpose(1, 0, 2),
        routes[0, 0],
        gates[0, 0],
        queries[0, 0],
        out_grad[0, 0],
        grads[0, 0],
        down_weight[0],
    )
    return (
        out[0].transpose(1, 0, 2)[None],
        out[1].transpose(1, 0, 2)[None, None],
        out[2][None, :, None],
    )


def solution(mesh):
    nx = 4 if mesh.shape["seq"] == 32 else 2
    placed = (
        P("expert", "seq", None, "mp"),
        P("expert", "seq", None, "mp"),
        P("expert", "seq", None, "mp"),
        P("expert", "seq", None, None, "mp"),
        P("expert", "seq"),
        P("expert", "seq", None, None),
        P("expert", "seq", None, None),
        P("expert", "seq", None, None),
        P("expert", "mp", None),
    )
    return jax.shard_map(
        functools.partial(local, nx),
        mesh=mesh,
        in_specs=placed,
        out_specs=(
            P("expert", "seq", None, "mp"),
            P("expert", "seq", None, None, "mp"),
            P("seq", None, "expert", None, "mp"),
        ),
        check_vma=False,
    )
```

```python
import functools
import math

import jax
import jax.numpy as jnp
from jax import lax
from jax.experimental import pallas as pl
from jax.experimental.pallas import tpu as pltpu
from jax.sharding import PartitionSpec as P

HD = 128
SCALE = HD**-0.5
SCALE2 = SCALE * math.log2(math.e)
MESH = pl.DeviceIdType.MESH
F32 = jnp.float32
BF16 = jnp.bfloat16
NT = (((1,), (1,)), ((), ()))
NN = (((1,), (0,)), ((), ()))
TILE = 512


def kernel(
    nx,
    nz,
    len_ref,
    pkv_ref,
    rkv_ref,
    routes_ref,
    gates_ref,
    q_hbm,
    g_hbm,
    tok_hbm,
    w_hbm,
    pout,
    rout,
    eout,
    q,
    g,
    tok,
    w,
    gath,
    num,
    prob,
    stat,
    low_a,
    low_g,
    part1,
    recv1,
    own_sum,
    part2,
    recv2,
    rows_out,
    rows_in,
    own_grad,
    own_prompt,
    hid,
    local_sem,
    zs,
    zr,
    xs,
    xr,
    es,
    er,
    cs,
    cr,
    s1,
    r1,
    s2,
    r2,
):
    seq = lax.axis_index("seq")
    me_e = lax.axis_index("expert")
    me_c = lax.axis_index("mp")
    me_x, me_z = seq // nz, seq % nz
    ne = rows_out.shape[0]
    cap = rows_out.shape[1]
    half = rows_out.shape[2]
    rows_all = q.shape[0]
    heads = rows_all // 128
    toks = gath.shape[3]
    blk = nz * toks

    def at_x(o):
        return {"seq": (me_x + o) % nx * nz + me_z}

    def at_z(o):
        return {"seq": me_x * nz + (me_z + o) % nz}

    def at_e(o):
        return {"expert": (me_e + o) % ne}

    sibling = {"mp": 1 - me_c}

    barrier = pltpu.get_barrier_semaphore()
    peers = [at_x(o) for o in range(1, nx)] + [at_z(o) for o in range(1, nz)]
    peers += [at_e(o) for o in range(1, ne)] + [sibling]
    for peer in peers:
        pl.semaphore_signal(barrier, inc=1, device_id=peer, device_id_type=MESH)

    tok_copy = pltpu.make_async_copy(
        tok_hbm.at[:, pl.ds(pl.multiple_of(me_c * half, half), half)], tok, local_sem.at[2]
    )
    tok_copy.start()
    for h in range(heads):
        cols = slice(h * HD, (h + 1) * HD)
        pltpu.make_async_copy(q_hbm.at[:, cols], q.at[h * 128 : (h + 1) * 128], local_sem.at[0]).start()
        pltpu.make_async_copy(g_hbm.at[:, cols], g.at[h * 128 : (h + 1) * 128], local_sem.at[1]).start()
    w_copy = pltpu.make_async_copy(w_hbm, w, local_sem.at[3])
    w_copy.start()
    gath[me_x, me_z, 0] = pkv_ref[:, 0, :]
    gath[me_x, me_z, 1] = pkv_ref[:, 1, :]
    pl.semaphore_wait(barrier, len(peers))

    sends = []

    def remote(src, dst, send_sem, recv_sem, peer):
        copy = pltpu.make_async_remote_copy(
            src_ref=src,
            dst_ref=dst,
            send_sem=send_sem,
            recv_sem=recv_sem,
            device_id=peer,
            device_id_type=MESH,
        )
        copy.start()
        sends.append(copy)

    z_order = sorted(range(1, nz), key=lambda o: min(o, nz - o))
    own_block = gath.at[me_x, me_z]
    for o in reversed(z_order):
        remote(own_block, own_block, zs.at[o - 1], zr.at[me_z], at_z(o))

    def forward(k, zb):
        block = gath.at[me_x, zb]
        for o in range(1, nx):
            remote(block, block, xs.at[o - 1, k], xr.at[o - 1], at_x(o))

    forward(0, me_z)

    length = len_ref[0, 0]
    lane = lax.broadcasted_iota(jnp.int32, (1, 128), 1)
    route_t = routes_ref[...].astype(F32)
    gate_t = gates_ref[...]
    valid = (lane < length).astype(F32)
    named, weight = [], []
    for e in range(ne):
        hit = route_t == float(e)
        named.append(jnp.max(hit.astype(F32), 0, keepdims=True))
        weight.append(jnp.sum(jnp.where(hit, gate_t, 0.0), 0, keepdims=True) * valid)
    named_all = jnp.concatenate(named, 0)
    upper = (
        lax.broadcasted_iota(jnp.int32, (128, 128), 0) <= lax.broadcasted_iota(jnp.int32, (128, 128), 1)
    ).astype(BF16)
    slot = lax.dot_general(named_all.astype(BF16), upper, NN, preferred_element_type=F32) - 1.0
    slot_id = lax.broadcasted_iota(jnp.int32, (cap, 128), 0).astype(F32)
    select, slot_gate = [], []
    for e in range(ne):
        chosen = jnp.where(slot[e : e + 1] == slot_id, named[e], 0.0)
        select.append(chosen)
        slot_gate.append(jnp.sum(chosen * weight[e], 1, keepdims=True))
    select = jnp.concatenate(select, 0).astype(BF16)
    slot_gate = jnp.concatenate(slot_gate, 0)
    tok_copy.wait()
    picked = lax.dot_general(select, tok[...], NN, preferred_element_type=F32)
    rows_out[...] = (picked * slot_gate).astype(BF16).reshape(ne, cap, half)

    pltpu.make_async_copy(q, q, local_sem.at[0]).wait()
    pltpu.make_async_copy(g, g, local_sem.at[1]).wait()
    row_at = lax.broadcasted_iota(jnp.int32, (128, HD), 0)
    for h in range(heads):
        part = g[h * 128 : (h + 1) * 128, :]
        g[h * 128 : (h + 1) * 128, :] = jnp.where(row_at < length, part.astype(F32), 0.0).astype(BF16)

    def forward_block(b, keys, values, causal):
        n = keys.shape[0]
        for t in range(rows_all // TILE):
            rows = slice(t * TILE, (t + 1) * TILE)
            score = lax.dot_general(keys, q[rows, :], NT, preferred_element_type=F32)
            if causal:
                key_at = lax.broadcasted_iota(jnp.int32, (n, TILE), 0)
                query_at = lax.broadcasted_iota(jnp.int32, (n, TILE), 1) % 128
                score = jnp.where(key_at <= query_at, score, -jnp.inf)
            top = jnp.max(score, 0, keepdims=True)
            exps = jnp.exp2((score - top) * SCALE2)
            probs = lax.dot_general(values, g[rows, :], NT, preferred_element_type=F32)
            stat[0, b : b + 1, rows] = top
            stat[1, b : b + 1, rows] = jnp.sum(exps, 0, keepdims=True)
            stat[2, b : b + 1, rows] = jnp.sum(exps * probs, 0, keepdims=True)
            num[b, 0:n, rows] = exps
            prob[b, 0:n, rows] = probs

    own_b = nx
    forward_block(own_b, rkv_ref[:, 0, :], rkv_ref[:, 1, :], True)

    for k, o in enumerate(z_order):
        zb = (me_z + o) % nz
        block = gath.at[me_x, zb]
        pltpu.make_async_copy(block, block, zr.at[zb]).wait()
        forward(k + 1, zb)

    for o in range(1, ne):
        there = (me_e + o) % ne
        remote(rows_out.at[there], rows_in.at[me_c, me_e], es.at[o - 1], er.at[me_e], at_e(o))
    rows_in[me_c, me_e] = rows_out[me_e]

    x_order = sorted(range(1, nx), key=lambda o: min(o, nx - o))
    for b, o in enumerate([0] + x_order):
        xb = (me_x + nx - o) % nx
        if o:
            came = gath.at[xb]
            pltpu.make_async_copy(came, came, xr.at[o - 1]).wait()
        forward_block(
            b, gath[xb, :, 0].reshape(blk, HD), gath[xb, :, 1].reshape(blk, HD), False
        )

    nb = nx + 1
    top = stat[0, 0:nb, :]
    factor = jnp.exp2((top - jnp.max(top, 0, keepdims=True)) * SCALE2)
    inverse = 1.0 / jnp.sum(stat[1, 0:nb, :] * factor, 0, keepdims=True)
    delta = jnp.sum(stat[2, 0:nb, :] * factor, 0, keepdims=True) * inverse
    stat[0, 0:nb, :] = factor * inverse
    stat[1, 0:1, :] = delta

    def backward_block(b, keys, n):
        for t in range(rows_all // 256):
            rows = slice(t * 256, (t + 1) * 256)
            attention = num[b, keys, rows] * stat[0, b : b + 1, rows]
            grad = attention * ((prob[b, keys, rows] - stat[1, 0:1, rows]) * SCALE)
            low_a[0:n, rows] = attention.astype(BF16)
            low_g[0:n, rows] = grad.astype(BF16)
        grad_v = lax.dot_general(low_a[0:n, :], g[...], NN, preferred_element_type=F32)
        grad_k = lax.dot_general(low_g[0:n, :], q[...], NN, preferred_element_type=F32)
        return grad_k, grad_v

    hz = nz // 2
    sub = hz * toks
    my_half, my_at = me_z // hz, me_z % hz
    halves = [1 - my_half, my_half]
    for step in range(2):
        keys = pl.ds(pl.multiple_of(halves[step] * sub, sub), sub)
        for b, o in reversed(list(enumerate([0] + x_order))):
            grad_k, grad_v = backward_block(b, keys, sub)
            if o:
                part1[b - 1, step, 0] = grad_k.astype(BF16)
                part1[b - 1, step, 1] = grad_v.astype(BF16)
                remote(
                    part1.at[b - 1, step],
                    recv1.at[o - 1, step],
                    s1.at[o - 1, step],
                    r1.at[o - 1, step],
                    at_x(nx - o),
                )
            else:
                own_sum[step, 0] = grad_k
                own_sum[step, 1] = grad_v

    grad_k, grad_v = backward_block(own_b, slice(0, 128), 128)
    own_grad[0] = grad_k
    own_grad[1] = grad_v
    own_out = pltpu.make_async_copy(own_grad, rout, local_sem.at[4])
    own_out.start()

    for step in range(2):
        for o in range(1, nx):
            came = recv1.at[o - 1, step]
            pltpu.make_async_copy(came, came, r1.at[o - 1, step]).wait()
        for j in range(hz):
            keys = slice(j * toks, (j + 1) * toks)
            for kv in range(2):
                total = own_sum[step, kv, keys, :]
                for o in range(1, nx):
                    total = total + recv1[o - 1, step, kv, keys, :].astype(F32)
                own_sum[step, kv, keys, :] = total
                part2[step, j, kv] = total.astype(BF16)
        for o in range(step, hz):
            j = (my_at + o) % hz
            remote(
                part2.at[step, j],
                recv2.at[me_z],
                s2.at[step * hz + o],
                r2.at[me_z],
                {"seq": me_x * nz + halves[step] * hz + j},
            )

    for o in range(1, ne):
        there = (me_e + o) % ne
        came = rows_in.at[me_c, there]
        pltpu.make_async_copy(came, came, er.at[there]).wait()
    remote(rows_in.at[me_c], rows_in.at[me_c], cs.at[0], cr.at[0], sibling)

    w_copy.wait()
    other = rows_in.at[1 - me_c]
    pltpu.make_async_copy(other, other, cr.at[0]).wait()
    hidden = lax.dot_general(
        rows_in[0].reshape(ne * cap, half), w[:, 0:half], NT, preferred_element_type=F32
    )
    hidden = hidden + lax.dot_general(
        rows_in[1].reshape(ne * cap, half), w[:, half : 2 * half], NT, preferred_element_type=F32
    )
    hid[...] = hidden.astype(BF16).reshape(hid.shape)
    hid_out = pltpu.make_async_copy(hid, eout, local_sem.at[5])
    hid_out.start()

    mine = pl.ds(pl.multiple_of(my_at * toks, toks), toks)
    total_k, total_v = own_sum[1, 0, mine, :], own_sum[1, 1, mine, :]
    for o in z_order:
        zb = (me_z + o) % nz
        came = recv2.at[zb]
        pltpu.make_async_copy(came, came, r2.at[zb]).wait()
        total_k = total_k + recv2[zb, 0].astype(F32)
        total_v = total_v + recv2[zb, 1].astype(F32)
    own_prompt[0] = total_k
    own_prompt[1] = total_v
    prompt_out = pltpu.make_async_copy(own_prompt, pout, local_sem.at[6])
    prompt_out.start()
    own_out.wait()
    hid_out.wait()
    prompt_out.wait()
    for copy in sends:
        copy.wait_send()


def place(pin, rin, ein, pout, rout, eout, sem):
    copies = [
        pltpu.make_async_copy(pin.at[0], pout.at[:, 0, :], sem.at[0]),
        pltpu.make_async_copy(pin.at[1], pout.at[:, 1, :], sem.at[1]),
        pltpu.make_async_copy(rin.at[0], rout.at[:, 0, :], sem.at[2]),
        pltpu.make_async_copy(rin.at[1], rout.at[:, 1, :], sem.at[3]),
        pltpu.make_async_copy(ein, eout, sem.at[4]),
    ]
    for copy in copies:
        copy.start()
    for copy in copies:
        copy.wait()


def local(nx, queries, out_grad, prompt_kv, resp_kv, lengths, grads, routes, gates, down_weight):
    ne = lax.axis_size("expert")
    toks = prompt_kv.shape[1]
    rows = queries.shape[2]
    width = queries.shape[3]
    heads = width // HD
    nz = lax.axis_size("seq") // nx
    features = grads.shape[3]
    half = features // 2
    hidden = down_weight.shape[1]
    cap = rows // 8
    blk = nz * toks
    vmem = pl.BlockSpec(memory_space=pltpu.VMEM)
    hbm = pl.BlockSpec(memory_space=pl.ANY)
    dma = pltpu.SemaphoreType.DMA
    out = pl.pallas_call(
        functools.partial(kernel, nx, nz),
        out_shape=[
            jax.ShapeDtypeStruct((2, toks, HD), F32),
            jax.ShapeDtypeStruct((2, rows, HD), F32),
            jax.ShapeDtypeStruct((ne, cap, hidden), BF16),
        ],
        in_specs=[pl.BlockSpec(memory_space=pltpu.SMEM)] + [vmem] * 4 + [hbm] * 4,
        out_specs=[hbm] * 3,
        scratch_shapes=[
            pltpu.VMEM((heads * rows, HD), BF16),
            pltpu.VMEM((heads * rows, HD), BF16),
            pltpu.VMEM((rows, half), BF16),
            pltpu.VMEM((hidden, features), BF16),
            pltpu.VMEM((nx, nz, 2, toks, HD), BF16),
            pltpu.VMEM((nx + 1, max(blk, rows), heads * rows), F32),
            pltpu.VMEM((nx + 1, max(blk, rows), heads * rows), F32),
            pltpu.VMEM((3, 8, heads * rows), F32),
            pltpu.VMEM((128, heads * rows), BF16),
            pltpu.VMEM((128, heads * rows), BF16),
            pltpu.VMEM((nx - 1, 2, 2, blk // 2, HD), BF16),
            pltpu.VMEM((nx - 1, 2, 2, blk // 2, HD), BF16),
            pltpu.VMEM((2, 2, blk // 2, HD), F32),
            pltpu.VMEM((2, nz // 2, 2, toks, HD), BF16),
            pltpu.VMEM((nz, 2, toks, HD), BF16),
            pltpu.VMEM((ne, cap, half), BF16),
            pltpu.VMEM((2, ne, cap, half), BF16),
            pltpu.VMEM((2, rows, HD), F32),
            pltpu.VMEM((2, toks, HD), F32),
            pltpu.VMEM((ne, cap, hidden), BF16),
            dma((7,)),
            dma((nz - 1,)),
            dma((nz,)),
            dma((nx - 1, nz)),
            dma((nx - 1,)),
            dma((ne - 1,)),
            dma((ne,)),
            dma((1,)),
            dma((1,)),
            dma((nx - 1, 2)),
            dma((nx - 1, 2)),
            dma((nz,)),
            dma((nz,)),
        ],
        compiler_params=pltpu.CompilerParams(
            collective_id=0, has_side_effects=True, vmem_limit_bytes=60 << 20
        ),
        name="moe_attention_backward",
    )(
        lengths,
        prompt_kv[0],
        resp_kv[0, 0],
        routes[0, 0].T,
        gates[0, 0].T,
        queries[0, 0],
        out_grad[0, 0],
        grads[0, 0],
        down_weight[0],
    )
    placed = pl.pallas_call(
        place,
        out_shape=[
            jax.ShapeDtypeStruct((toks, 2, HD), F32),
            jax.ShapeDtypeStruct((rows, 2, HD), F32),
            jax.ShapeDtypeStruct((ne, cap, hidden), BF16),
        ],
        in_specs=[hbm] * 3,
        out_specs=[hbm] * 3,
        scratch_shapes=[dma((5,))],
        compiler_params=pltpu.CompilerParams(vmem_limit_bytes=60 << 20),
        name="place_outputs",
    )(*out)
    return (placed[0][None], placed[1][None, None], placed[2][None, :, None])


def solution(mesh):
    nx = 4 if mesh.shape["seq"] == 32 else 2
    placed = (
        P("expert", "seq", None, "mp"),
        P("expert", "seq", None, "mp"),
        P("expert", "seq", None, "mp"),
        P("expert", "seq", None, None, "mp"),
        P("expert", "seq"),
        P("expert", "seq", None, None),
        P("expert", "seq", None, None),
        P("expert", "seq", None, None),
        P("expert", "mp", None),
    )
    return jax.shard_map(
        functools.partial(local, nx),
        mesh=mesh,
        in_specs=placed,
        out_specs=(
            P("expert", "seq", None, "mp"),
            P("expert", "seq", None, None, "mp"),
            P("seq", None, "expert", None, "mp"),
        ),
        check_vma=False,
    )
```

```python
import functools
import math

import jax
import jax.numpy as jnp
from jax import lax
from jax.experimental import pallas as pl
from jax.experimental.pallas import tpu as pltpu
from jax.sharding import PartitionSpec as P

HD = 128
SCALE = HD**-0.5
SCALE2 = SCALE * math.log2(math.e)
MESH = pl.DeviceIdType.MESH
F32 = jnp.float32
BF16 = jnp.bfloat16
NT = (((1,), (1,)), ((), ()))
NN = (((1,), (0,)), ((), ()))
TILE = 512


def kernel(
    nx,
    nz,
    len_ref,
    pkv_ref,
    rkv_ref,
    routes_ref,
    gates_ref,
    q_hbm,
    g_hbm,
    tok_hbm,
    w_hbm,
    pout,
    rout,
    eout,
    q,
    g,
    tok,
    w,
    gath,
    num,
    prob,
    stat,
    low_a,
    low_g,
    part1,
    recv1,
    own_sum,
    part2,
    recv2,
    rows_out,
    rows_in,
    own_grad,
    own_prompt,
    hid,
    local_sem,
    zs,
    zr,
    xs,
    xr,
    es,
    er,
    cs,
    cr,
    s1,
    r1,
    s2,
    r2,
    ready,
):
    seq = lax.axis_index("seq")
    me_e = lax.axis_index("expert")
    me_c = lax.axis_index("mp")
    me_x, me_z = seq // nz, seq % nz
    ne = rows_out.shape[0]
    cap = rows_out.shape[1]
    half = rows_out.shape[2]
    rows_all = q.shape[0]
    heads = rows_all // 128
    toks = gath.shape[3]
    blk = nz * toks

    def at_x(o):
        return {"seq": (me_x + o) % nx * nz + me_z}

    def at_z(o):
        return {"seq": me_x * nz + (me_z + o) % nz}

    ny = ne // 2
    me_h, me_y = me_e // ny, me_e % ny

    def at_y(o):
        return me_h * ny + (me_y + o) % ny

    def far(o):
        return (1 - me_h) * ny + (me_y + o) % ny

    sibling = {"mp": 1 - me_c}

    barrier = pltpu.get_barrier_semaphore()
    peers = [at_x(o) for o in range(1, nx)] + [at_z(o) for o in range(1, nz)]
    peers += [{"expert": at_y(o)} for o in range(1, ny)] + [sibling]

    @pl.when(me_h == 0)
    def _():
        for o in range(ny):
            pl.semaphore_signal(barrier, inc=1, device_id={"expert": far(o)}, device_id_type=MESH)

    for peer in peers:
        pl.semaphore_signal(barrier, inc=1, device_id=peer, device_id_type=MESH)

    tok_copy = pltpu.make_async_copy(
        tok_hbm.at[:, pl.ds(pl.multiple_of(me_c * half, half), half)], tok, local_sem.at[2]
    )
    tok_copy.start()
    for h in range(heads):
        cols = slice(h * HD, (h + 1) * HD)
        pltpu.make_async_copy(q_hbm.at[:, cols], q.at[h * 128 : (h + 1) * 128], local_sem.at[0]).start()
        pltpu.make_async_copy(g_hbm.at[:, cols], g.at[h * 128 : (h + 1) * 128], local_sem.at[1]).start()
    w_copy = pltpu.make_async_copy(w_hbm, w, local_sem.at[3])
    w_copy.start()
    gath[me_x, me_z, 0] = pkv_ref[:, 0, :]
    gath[me_x, me_z, 1] = pkv_ref[:, 1, :]
    pl.semaphore_wait(barrier, len(peers) + me_h * ny)

    @pl.when(me_h == 1)
    def _():
        for o in range(ny):
            pl.semaphore_signal(ready, inc=1, device_id={"expert": far(o)}, device_id_type=MESH)


    sends = []

    def remote(src, dst, send_sem, recv_sem, peer):
        copy = pltpu.make_async_remote_copy(
            src_ref=src,
            dst_ref=dst,
            send_sem=send_sem,
            recv_sem=recv_sem,
            device_id=peer,
            device_id_type=MESH,
        )
        copy.start()
        sends.append(copy)

    z_order = sorted(range(1, nz), key=lambda o: min(o, nz - o))
    own_block = gath.at[me_x, me_z]
    for o in reversed(z_order):
        remote(own_block, own_block, zs.at[o - 1], zr.at[me_z], at_z(o))

    def forward(k, zb):
        block = gath.at[me_x, zb]
        for o in range(1, nx):
            remote(block, block, xs.at[o - 1, k], xr.at[o - 1], at_x(o))

    forward(0, me_z)

    length = len_ref[0, 0]
    lane = lax.broadcasted_iota(jnp.int32, (1, 128), 1)
    route_t = routes_ref[...].astype(F32)
    gate_t = gates_ref[...]
    valid = (lane < length).astype(F32)
    named, weight = [], []
    for e in range(ne):
        hit = route_t == float(e)
        named.append(jnp.max(hit.astype(F32), 0, keepdims=True))
        weight.append(jnp.sum(jnp.where(hit, gate_t, 0.0), 0, keepdims=True) * valid)
    named_all = jnp.concatenate(named, 0)
    upper = (
        lax.broadcasted_iota(jnp.int32, (128, 128), 0) <= lax.broadcasted_iota(jnp.int32, (128, 128), 1)
    ).astype(BF16)
    slot = lax.dot_general(named_all.astype(BF16), upper, NN, preferred_element_type=F32) - 1.0
    slot_id = lax.broadcasted_iota(jnp.int32, (cap, 128), 0).astype(F32)
    select, slot_gate = [], []
    for e in range(ne):
        chosen = jnp.where(slot[e : e + 1] == slot_id, named[e], 0.0)
        select.append(chosen)
        slot_gate.append(jnp.sum(chosen * weight[e], 1, keepdims=True))
    select = jnp.concatenate(select, 0).astype(BF16)
    slot_gate = jnp.concatenate(slot_gate, 0)
    tok_copy.wait()
    picked = lax.dot_general(select, tok[...], NN, preferred_element_type=F32)
    rows_out[...] = (picked * slot_gate).astype(BF16).reshape(ne, cap, half)

    pltpu.make_async_copy(q, q, local_sem.at[0]).wait()
    pltpu.make_async_copy(g, g, local_sem.at[1]).wait()
    row_at = lax.broadcasted_iota(jnp.int32, (128, HD), 0)
    for h in range(heads):
        part = g[h * 128 : (h + 1) * 128, :]
        g[h * 128 : (h + 1) * 128, :] = jnp.where(row_at < length, part.astype(F32), 0.0).astype(BF16)

    def forward_block(b, keys, values, causal):
        n = keys.shape[0]
        for t in range(rows_all // TILE):
            rows = slice(t * TILE, (t + 1) * TILE)
            score = lax.dot_general(keys, q[rows, :], NT, preferred_element_type=F32)
            if causal:
                key_at = lax.broadcasted_iota(jnp.int32, (n, TILE), 0)
                query_at = lax.broadcasted_iota(jnp.int32, (n, TILE), 1) % 128
                score = jnp.where(key_at <= query_at, score, -jnp.inf)
            top = jnp.max(score, 0, keepdims=True)
            exps = jnp.exp2((score - top) * SCALE2)
            probs = lax.dot_general(values, g[rows, :], NT, preferred_element_type=F32)
            stat[0, b : b + 1, rows] = top
            stat[1, b : b + 1, rows] = jnp.sum(exps, 0, keepdims=True)
            stat[2, b : b + 1, rows] = jnp.sum(exps * probs, 0, keepdims=True)
            num[b, 0:n, rows] = exps
            prob[b, 0:n, rows] = probs

    own_b = nx
    forward_block(own_b, rkv_ref[:, 0, :], rkv_ref[:, 1, :], True)

    for k, o in enumerate(z_order):
        zb = (me_z + o) % nz
        block = gath.at[me_x, zb]
        pltpu.make_async_copy(block, block, zr.at[zb]).wait()
        forward(k + 1, zb)

    def routed(there, k):
        return pltpu.make_async_remote_copy(
            src_ref=rows_out.at[there],
            dst_ref=rows_in.at[me_c, me_e],
            send_sem=es.at[k],
            recv_sem=er.at[me_e],
            device_id={"expert": there},
            device_id_type=MESH,
        )

    near_rows = [routed(at_y(o), o - 1) for o in range(1, ny)]
    far_rows = [routed(far(o), ny - 1 + o) for o in range(ny)]

    @pl.when(me_h == 1)
    def _():
        for copy in far_rows:
            copy.start()

    for copy in near_rows:
        copy.start()
    rows_in[me_c, me_e] = rows_out[me_e]

    x_order = sorted(range(1, nx), key=lambda o: min(o, nx - o))
    for b, o in enumerate([0] + x_order):
        xb = (me_x + nx - o) % nx
        if o:
            came = gath.at[xb]
            pltpu.make_async_copy(came, came, xr.at[o - 1]).wait()
        forward_block(
            b, gath[xb, :, 0].reshape(blk, HD), gath[xb, :, 1].reshape(blk, HD), False
        )

    nb = nx + 1
    top = stat[0, 0:nb, :]
    factor = jnp.exp2((top - jnp.max(top, 0, keepdims=True)) * SCALE2)
    inverse = 1.0 / jnp.sum(stat[1, 0:nb, :] * factor, 0, keepdims=True)
    delta = jnp.sum(stat[2, 0:nb, :] * factor, 0, keepdims=True) * inverse
    stat[0, 0:nb, :] = factor * inverse
    stat[1, 0:1, :] = delta

    @pl.when(me_h == 0)
    def _():
        pl.semaphore_wait(ready, ny)
        for copy in far_rows:
            copy.start()

    def backward_block(b, keys, n):
        for t in range(rows_all // 256):
            rows = slice(t * 256, (t + 1) * 256)
            attention = num[b, keys, rows] * stat[0, b : b + 1, rows]
            grad = attention * ((prob[b, keys, rows] - stat[1, 0:1, rows]) * SCALE)
            low_a[0:n, rows] = attention.astype(BF16)
            low_g[0:n, rows] = grad.astype(BF16)
        grad_v = lax.dot_general(low_a[0:n, :], g[...], NN, preferred_element_type=F32)
        grad_k = lax.dot_general(low_g[0:n, :], q[...], NN, preferred_element_type=F32)
        return grad_k, grad_v

    hz = nz // 2
    sub = hz * toks
    my_half, my_at = me_z // hz, me_z % hz
    halves = [1 - my_half, my_half]
    for step in range(2):
        keys = pl.ds(pl.multiple_of(halves[step] * sub, sub), sub)
        for b, o in reversed(list(enumerate([0] + x_order))):
            grad_k, grad_v = backward_block(b, keys, sub)
            if o:
                part1[b - 1, step, 0] = grad_k.astype(BF16)
                part1[b - 1, step, 1] = grad_v.astype(BF16)
                remote(
                    part1.at[b - 1, step],
                    recv1.at[o - 1, step],
                    s1.at[o - 1, step],
                    r1.at[o - 1, step],
                    at_x(nx - o),
                )
            else:
                own_sum[step, 0] = grad_k
                own_sum[step, 1] = grad_v

    grad_k, grad_v = backward_block(own_b, slice(0, 128), 128)
    own_grad[0] = grad_k
    own_grad[1] = grad_v
    own_out = pltpu.make_async_copy(own_grad, rout, local_sem.at[4])
    own_out.start()

    for step in range(2):
        for o in range(1, nx):
            came = recv1.at[o - 1, step]
            pltpu.make_async_copy(came, came, r1.at[o - 1, step]).wait()
        for j in range(hz):
            keys = slice(j * toks, (j + 1) * toks)
            for kv in range(2):
                total = own_sum[step, kv, keys, :]
                for o in range(1, nx):
                    total = total + recv1[o - 1, step, kv, keys, :].astype(F32)
                own_sum[step, kv, keys, :] = total
                part2[step, j, kv] = total.astype(BF16)
        for o in range(step, hz):
            j = (my_at + o) % hz
            remote(
                part2.at[step, j],
                recv2.at[me_z],
                s2.at[step * hz + o],
                r2.at[me_z],
                {"seq": me_x * nz + halves[step] * hz + j},
            )

    for o in range(1, ne):
        there = (me_e + o) % ne
        came = rows_in.at[me_c, there]
        pltpu.make_async_copy(came, came, er.at[there]).wait()
    remote(rows_in.at[me_c], rows_in.at[me_c], cs.at[0], cr.at[0], sibling)

    w_copy.wait()
    other = rows_in.at[1 - me_c]
    pltpu.make_async_copy(other, other, cr.at[0]).wait()
    hidden = lax.dot_general(
        rows_in[0].reshape(ne * cap, half), w[:, 0:half], NT, preferred_element_type=F32
    )
    hidden = hidden + lax.dot_general(
        rows_in[1].reshape(ne * cap, half), w[:, half : 2 * half], NT, preferred_element_type=F32
    )
    hid[...] = hidden.astype(BF16).reshape(hid.shape)
    hid_out = pltpu.make_async_copy(hid, eout, local_sem.at[5])
    hid_out.start()

    mine = pl.ds(pl.multiple_of(my_at * toks, toks), toks)
    total_k, total_v = own_sum[1, 0, mine, :], own_sum[1, 1, mine, :]
    for o in z_order:
        zb = (me_z + o) % nz
        came = recv2.at[zb]
        pltpu.make_async_copy(came, came, r2.at[zb]).wait()
        total_k = total_k + recv2[zb, 0].astype(F32)
        total_v = total_v + recv2[zb, 1].astype(F32)
    own_prompt[0] = total_k
    own_prompt[1] = total_v
    prompt_out = pltpu.make_async_copy(own_prompt, pout, local_sem.at[6])
    prompt_out.start()
    own_out.wait()
    hid_out.wait()
    prompt_out.wait()
    for copy in sends + near_rows + far_rows:
        copy.wait_send()


def place(pin, rin, ein, pout, rout, eout):
    for kv in range(2):
        pout[:, kv, :] = pin[kv]
        rout[:, kv, :] = rin[kv]
    eout[...] = ein[...]


def local(nx, queries, out_grad, prompt_kv, resp_kv, lengths, grads, routes, gates, down_weight):
    ne = lax.axis_size("expert")
    toks = prompt_kv.shape[1]
    rows = queries.shape[2]
    width = queries.shape[3]
    heads = width // HD
    nz = lax.axis_size("seq") // nx
    features = grads.shape[3]
    half = features // 2
    hidden = down_weight.shape[1]
    cap = rows // 8
    blk = nz * toks
    vmem = pl.BlockSpec(memory_space=pltpu.VMEM)
    hbm = pl.BlockSpec(memory_space=pl.ANY)
    dma = pltpu.SemaphoreType.DMA
    out = pl.pallas_call(
        functools.partial(kernel, nx, nz),
        out_shape=[
            jax.ShapeDtypeStruct((2, toks, HD), F32),
            jax.ShapeDtypeStruct((2, rows, HD), F32),
            jax.ShapeDtypeStruct((ne, cap, hidden), BF16),
        ],
        in_specs=[pl.BlockSpec(memory_space=pltpu.SMEM)] + [vmem] * 4 + [hbm] * 4,
        out_specs=[hbm] * 3,
        scratch_shapes=[
            pltpu.VMEM((heads * rows, HD), BF16),
            pltpu.VMEM((heads * rows, HD), BF16),
            pltpu.VMEM((rows, half), BF16),
            pltpu.VMEM((hidden, features), BF16),
            pltpu.VMEM((nx, nz, 2, toks, HD), BF16),
            pltpu.VMEM((nx + 1, max(blk, rows), heads * rows), F32),
            pltpu.VMEM((nx + 1, max(blk, rows), heads * rows), F32),
            pltpu.VMEM((3, 8, heads * rows), F32),
            pltpu.VMEM((128, heads * rows), BF16),
            pltpu.VMEM((128, heads * rows), BF16),
            pltpu.VMEM((nx - 1, 2, 2, blk // 2, HD), BF16),
            pltpu.VMEM((nx - 1, 2, 2, blk // 2, HD), BF16),
            pltpu.VMEM((2, 2, blk // 2, HD), F32),
            pltpu.VMEM((2, nz // 2, 2, toks, HD), BF16),
            pltpu.VMEM((nz, 2, toks, HD), BF16),
            pltpu.VMEM((ne, cap, half), BF16),
            pltpu.VMEM((2, ne, cap, half), BF16),
            pltpu.VMEM((2, rows, HD), F32),
            pltpu.VMEM((2, toks, HD), F32),
            pltpu.VMEM((ne, cap, hidden), BF16),
            dma((7,)),
            dma((nz - 1,)),
            dma((nz,)),
            dma((nx - 1, nz)),
            dma((nx - 1,)),
            dma((ne - 1,)),
            dma((ne,)),
            dma((1,)),
            dma((1,)),
            dma((nx - 1, 2)),
            dma((nx - 1, 2)),
            dma((nz,)),
            dma((nz,)),
            pltpu.SemaphoreType.REGULAR,
        ],
        compiler_params=pltpu.CompilerParams(
            collective_id=0, has_side_effects=True, vmem_limit_bytes=60 << 20
        ),
        name="moe_attention_backward",
    )(
        lengths,
        prompt_kv[0],
        resp_kv[0, 0],
        routes[0, 0].T,
        gates[0, 0].T,
        queries[0, 0],
        out_grad[0, 0],
        grads[0, 0],
        down_weight[0],
    )
    placed = pl.pallas_call(
        place,
        out_shape=[
            jax.ShapeDtypeStruct((toks, 2, HD), F32),
            jax.ShapeDtypeStruct((rows, 2, HD), F32),
            jax.ShapeDtypeStruct((ne, cap, hidden), BF16),
        ],
        in_specs=[vmem] * 3,
        out_specs=[vmem] * 3,
        compiler_params=pltpu.CompilerParams(vmem_limit_bytes=60 << 20),
        name="place_outputs",
    )(*out)
    return (placed[0][None], placed[1][None, None], placed[2][None, :, None])


def solution(mesh):
    nx = 4 if mesh.shape["seq"] == 32 else 2
    placed = (
        P("expert", "seq", None, "mp"),
        P("expert", "seq", None, "mp"),
        P("expert", "seq", None, "mp"),
        P("expert", "seq", None, None, "mp"),
        P("expert", "seq"),
        P("expert", "seq", None, None),
        P("expert", "seq", None, None),
        P("expert", "seq", None, None),
        P("expert", "mp", None),
    )
    return jax.shard_map(
        functools.partial(local, nx),
        mesh=mesh,
        in_specs=placed,
        out_specs=(
            P("expert", "seq", None, "mp"),
            P("expert", "seq", None, None, "mp"),
            P("seq", None, "expert", None, "mp"),
        ),
        check_vma=False,
    )
```

```python
import functools
import math

import jax
import jax.numpy as jnp
from jax import lax
from jax.experimental import pallas as pl
from jax.experimental.pallas import tpu as pltpu
from jax.sharding import PartitionSpec as P

HD = 128
SCALE = HD**-0.5
SCALE2 = SCALE * math.log2(math.e)
MESH = pl.DeviceIdType.MESH
F32 = jnp.float32
BF16 = jnp.bfloat16
NT = (((1,), (1,)), ((), ()))
NN = (((1,), (0,)), ((), ()))
TILE = 512


def kernel(
    nx,
    nz,
    len_ref,
    pkv_hbm,
    rkv_hbm,
    routes_hbm,
    gates_hbm,
    q_hbm,
    g_hbm,
    tok_hbm,
    w_hbm,
    pout,
    rout,
    eout,
    q,
    g,
    tok,
    w,
    gath,
    num,
    prob,
    stat,
    low_a,
    low_g,
    part1,
    recv1,
    own_sum,
    part2,
    recv2,
    rows_out,
    rows_in,
    own_grad,
    own_prompt,
    hid,
    pkv_ref,
    rkv_ref,
    routes_ref,
    gates_ref,
    local_sem,
    zs,
    zr,
    xs,
    xr,
    es,
    er,
    cs,
    cr,
    s1,
    r1,
    s2,
    r2,
    ready,
):
    seq = lax.axis_index("seq")
    me_e = lax.axis_index("expert")
    me_c = lax.axis_index("mp")
    me_x, me_z = seq // nz, seq % nz
    ne = rows_out.shape[0]
    cap = rows_out.shape[1]
    half = rows_out.shape[2]
    rows_all = q.shape[0]
    heads = rows_all // 128
    toks = gath.shape[3]
    blk = nz * toks

    def at_x(o):
        return {"seq": (me_x + o) % nx * nz + me_z}

    def at_z(o):
        return {"seq": me_x * nz + (me_z + o) % nz}

    ny = ne // 2
    me_h, me_y = me_e // ny, me_e % ny

    def at_y(o):
        return me_h * ny + (me_y + o) % ny

    def far(o):
        return (1 - me_h) * ny + (me_y + o) % ny

    sibling = {"mp": 1 - me_c}

    barrier = pltpu.get_barrier_semaphore()
    peers = [at_x(o) for o in range(1, nx)] + [at_z(o) for o in range(1, nz)]
    peers += [{"expert": at_y(o)} for o in range(1, ny)] + [sibling]

    @pl.when(me_h == 0)
    def _():
        for o in range(ny):
            pl.semaphore_signal(barrier, inc=1, device_id={"expert": far(o)}, device_id_type=MESH)

    for peer in peers:
        pl.semaphore_signal(barrier, inc=1, device_id=peer, device_id_type=MESH)

    small = [
        pltpu.make_async_copy(src, dst, local_sem.at[7 + k])
        for k, (src, dst) in enumerate(
            [(pkv_hbm, pkv_ref), (routes_hbm, routes_ref), (gates_hbm, gates_ref), (rkv_hbm, rkv_ref)]
        )
    ]
    for copy in small:
        copy.start()
    tok_copy = pltpu.make_async_copy(
        tok_hbm.at[:, pl.ds(pl.multiple_of(me_c * half, half), half)], tok, local_sem.at[2]
    )
    tok_copy.start()
    for h in range(heads):
        cols = slice(h * HD, (h + 1) * HD)
        pltpu.make_async_copy(q_hbm.at[:, cols], q.at[h * 128 : (h + 1) * 128], local_sem.at[0]).start()
        pltpu.make_async_copy(g_hbm.at[:, cols], g.at[h * 128 : (h + 1) * 128], local_sem.at[1]).start()
    w_copy = pltpu.make_async_copy(w_hbm, w, local_sem.at[3])
    w_copy.start()
    small[0].wait()
    gath[me_x, me_z, 0] = pkv_ref[:, 0, :]
    gath[me_x, me_z, 1] = pkv_ref[:, 1, :]
    pl.semaphore_wait(barrier, len(peers) + me_h * ny)

    @pl.when(me_h == 1)
    def _():
        for o in range(ny):
            pl.semaphore_signal(ready, inc=1, device_id={"expert": far(o)}, device_id_type=MESH)


    sends = []

    def remote(src, dst, send_sem, recv_sem, peer):
        copy = pltpu.make_async_remote_copy(
            src_ref=src,
            dst_ref=dst,
            send_sem=send_sem,
            recv_sem=recv_sem,
            device_id=peer,
            device_id_type=MESH,
        )
        copy.start()
        sends.append(copy)

    z_order = sorted(range(1, nz), key=lambda o: min(o, nz - o))
    own_block = gath.at[me_x, me_z]
    for o in reversed(z_order):
        remote(own_block, own_block, zs.at[o - 1], zr.at[me_z], at_z(o))

    def forward(k, zb):
        block = gath.at[me_x, zb]
        for o in range(1, nx):
            remote(block, block, xs.at[o - 1, k], xr.at[o - 1], at_x(o))

    forward(0, me_z)

    length = len_ref[0, 0]
    lane = lax.broadcasted_iota(jnp.int32, (1, 128), 1)
    small[1].wait()
    small[2].wait()
    route_t = routes_ref[...].astype(F32)
    gate_t = gates_ref[...]
    valid = (lane < length).astype(F32)
    named, weight = [], []
    for e in range(ne):
        hit = route_t == float(e)
        named.append(jnp.max(hit.astype(F32), 0, keepdims=True))
        weight.append(jnp.sum(jnp.where(hit, gate_t, 0.0), 0, keepdims=True) * valid)
    named_all = jnp.concatenate(named, 0)
    upper = (
        lax.broadcasted_iota(jnp.int32, (128, 128), 0) <= lax.broadcasted_iota(jnp.int32, (128, 128), 1)
    ).astype(BF16)
    slot = lax.dot_general(named_all.astype(BF16), upper, NN, preferred_element_type=F32) - 1.0
    slot_id = lax.broadcasted_iota(jnp.int32, (cap, 128), 0).astype(F32)
    select, slot_gate = [], []
    for e in range(ne):
        chosen = jnp.where(slot[e : e + 1] == slot_id, named[e], 0.0)
        select.append(chosen)
        slot_gate.append(jnp.sum(chosen * weight[e], 1, keepdims=True))
    select = jnp.concatenate(select, 0).astype(BF16)
    slot_gate = jnp.concatenate(slot_gate, 0)
    tok_copy.wait()
    picked = lax.dot_general(select, tok[...], NN, preferred_element_type=F32)
    rows_out[...] = (picked * slot_gate).astype(BF16).reshape(ne, cap, half)

    pltpu.make_async_copy(q, q, local_sem.at[0]).wait()
    pltpu.make_async_copy(g, g, local_sem.at[1]).wait()
    row_at = lax.broadcasted_iota(jnp.int32, (128, HD), 0)
    for h in range(heads):
        part = g[h * 128 : (h + 1) * 128, :]
        g[h * 128 : (h + 1) * 128, :] = jnp.where(row_at < length, part.astype(F32), 0.0).astype(BF16)

    def forward_block(b, keys, values, causal):
        n = keys.shape[0]
        for t in range(rows_all // TILE):
            rows = slice(t * TILE, (t + 1) * TILE)
            score = lax.dot_general(keys, q[rows, :], NT, preferred_element_type=F32)
            if causal:
                key_at = lax.broadcasted_iota(jnp.int32, (n, TILE), 0)
                query_at = lax.broadcasted_iota(jnp.int32, (n, TILE), 1) % 128
                score = jnp.where(key_at <= query_at, score, -jnp.inf)
            top = jnp.max(score, 0, keepdims=True)
            exps = jnp.exp2((score - top) * SCALE2)
            probs = lax.dot_general(values, g[rows, :], NT, preferred_element_type=F32)
            stat[0, b : b + 1, rows] = top
            stat[1, b : b + 1, rows] = jnp.sum(exps, 0, keepdims=True)
            stat[2, b : b + 1, rows] = jnp.sum(exps * probs, 0, keepdims=True)
            num[b, 0:n, rows] = exps
            prob[b, 0:n, rows] = probs

    own_b = nx
    small[3].wait()
    forward_block(own_b, rkv_ref[:, 0, :], rkv_ref[:, 1, :], True)

    for k, o in enumerate(z_order):
        zb = (me_z + o) % nz
        block = gath.at[me_x, zb]
        pltpu.make_async_copy(block, block, zr.at[zb]).wait()
        forward(k + 1, zb)

    def routed(there, k):
        return pltpu.make_async_remote_copy(
            src_ref=rows_out.at[there],
            dst_ref=rows_in.at[me_c, me_e],
            send_sem=es.at[k],
            recv_sem=er.at[me_e],
            device_id={"expert": there},
            device_id_type=MESH,
        )

    near_rows = [routed(at_y(o), o - 1) for o in range(1, ny)]
    far_rows = [routed(far(o), ny - 1 + o) for o in range(ny)]

    @pl.when(me_h == 1)
    def _():
        for copy in far_rows:
            copy.start()

    for copy in near_rows:
        copy.start()
    rows_in[me_c, me_e] = rows_out[me_e]

    x_order = sorted(range(1, nx), key=lambda o: min(o, nx - o))
    for b, o in enumerate([0] + x_order):
        xb = (me_x + nx - o) % nx
        if o:
            came = gath.at[xb]
            pltpu.make_async_copy(came, came, xr.at[o - 1]).wait()
        forward_block(
            b, gath[xb, :, 0].reshape(blk, HD), gath[xb, :, 1].reshape(blk, HD), False
        )
        if b == 0:
            @pl.when(me_h == 0)
            def _():
                pl.semaphore_wait(ready, ny)
                for copy in far_rows:
                    copy.start()

    nb = nx + 1
    top = stat[0, 0:nb, :]
    factor = jnp.exp2((top - jnp.max(top, 0, keepdims=True)) * SCALE2)
    inverse = 1.0 / jnp.sum(stat[1, 0:nb, :] * factor, 0, keepdims=True)
    delta = jnp.sum(stat[2, 0:nb, :] * factor, 0, keepdims=True) * inverse
    stat[0, 0:nb, :] = factor * inverse
    stat[1, 0:1, :] = delta

    def backward_block(b, keys, n, at):
        for t in range(rows_all // 256):
            rows = slice(t * 256, (t + 1) * 256)
            attention = num[b, keys, rows] * stat[0, b : b + 1, rows]
            grad = attention * ((prob[b, keys, rows] - stat[1, 0:1, rows]) * SCALE)
            low_a[at, 0:n, rows] = attention.astype(BF16)
            low_g[at, 0:n, rows] = grad.astype(BF16)
        grad_v = lax.dot_general(low_a[at, 0:n, :], g[...], NN, preferred_element_type=F32)
        grad_k = lax.dot_general(low_g[at, 0:n, :], q[...], NN, preferred_element_type=F32)
        return grad_k, grad_v

    hz = nz // 2
    sub = hz * toks
    my_half, my_at = me_z // hz, me_z % hz
    halves = [1 - my_half, my_half]
    for step in range(2):
        keys = pl.ds(pl.multiple_of(halves[step] * sub, sub), sub)
        for b, o in reversed(list(enumerate([0] + x_order))):
            grad_k, grad_v = backward_block(b, keys, sub, b % 2)
            if o:
                part1[b - 1, step, 0] = grad_k.astype(BF16)
                part1[b - 1, step, 1] = grad_v.astype(BF16)
                remote(
                    part1.at[b - 1, step],
                    recv1.at[o - 1, step],
                    s1.at[o - 1, step],
                    r1.at[o - 1, step],
                    at_x(nx - o),
                )
            else:
                own_sum[step, 0] = grad_k
                own_sum[step, 1] = grad_v

    grad_k, grad_v = backward_block(own_b, slice(0, 128), 128, 1)
    own_grad[0] = grad_k
    own_grad[1] = grad_v
    own_out = pltpu.make_async_copy(own_grad, rout, local_sem.at[4])
    own_out.start()

    for step in range(2):
        for o in range(1, nx):
            came = recv1.at[o - 1, step]
            pltpu.make_async_copy(came, came, r1.at[o - 1, step]).wait()
        for j in range(hz):
            keys = slice(j * toks, (j + 1) * toks)
            for kv in range(2):
                total = own_sum[step, kv, keys, :]
                for o in range(1, nx):
                    total = total + recv1[o - 1, step, kv, keys, :].astype(F32)
                own_sum[step, kv, keys, :] = total
                part2[step, j, kv] = total.astype(BF16)
        for o in range(step, hz):
            j = (my_at + o) % hz
            remote(
                part2.at[step, j],
                recv2.at[me_z],
                s2.at[step * hz + o],
                r2.at[me_z],
                {"seq": me_x * nz + halves[step] * hz + j},
            )

    for o in range(1, ne):
        there = (me_e + o) % ne
        came = rows_in.at[me_c, there]
        pltpu.make_async_copy(came, came, er.at[there]).wait()
    remote(rows_in.at[me_c], rows_in.at[me_c], cs.at[0], cr.at[0], sibling)

    w_copy.wait()
    other = rows_in.at[1 - me_c]
    pltpu.make_async_copy(other, other, cr.at[0]).wait()
    hidden = lax.dot_general(
        rows_in[0].reshape(ne * cap, half), w[:, 0:half], NT, preferred_element_type=F32
    )
    hidden = hidden + lax.dot_general(
        rows_in[1].reshape(ne * cap, half), w[:, half : 2 * half], NT, preferred_element_type=F32
    )
    hid[...] = hidden.astype(BF16).reshape(hid.shape)
    hid_out = pltpu.make_async_copy(hid, eout, local_sem.at[5])
    hid_out.start()

    mine = pl.ds(pl.multiple_of(my_at * toks, toks), toks)
    total_k, total_v = own_sum[1, 0, mine, :], own_sum[1, 1, mine, :]
    for o in z_order:
        zb = (me_z + o) % nz
        came = recv2.at[zb]
        pltpu.make_async_copy(came, came, r2.at[zb]).wait()
        total_k = total_k + recv2[zb, 0].astype(F32)
        total_v = total_v + recv2[zb, 1].astype(F32)
    own_prompt[0] = total_k
    own_prompt[1] = total_v
    prompt_out = pltpu.make_async_copy(own_prompt, pout, local_sem.at[6])
    prompt_out.start()
    own_out.wait()
    hid_out.wait()
    prompt_out.wait()
    for copy in sends + near_rows + far_rows:
        copy.wait_send()


def place(pin, rin, ein, pout, rout, eout):
    for kv in range(2):
        pout[:, kv, :] = pin[kv]
        rout[:, kv, :] = rin[kv]
    eout[...] = ein[...]


def local(nx, queries, out_grad, prompt_kv, resp_kv, lengths, grads, routes, gates, down_weight):
    ne = lax.axis_size("expert")
    toks = prompt_kv.shape[1]
    rows = queries.shape[2]
    width = queries.shape[3]
    heads = width // HD
    nz = lax.axis_size("seq") // nx
    features = grads.shape[3]
    half = features // 2
    hidden = down_weight.shape[1]
    cap = rows // 8
    blk = nz * toks
    vmem = pl.BlockSpec(memory_space=pltpu.VMEM)
    hbm = pl.BlockSpec(memory_space=pl.ANY)
    dma = pltpu.SemaphoreType.DMA
    out = pl.pallas_call(
        functools.partial(kernel, nx, nz),
        out_shape=[
            jax.ShapeDtypeStruct((2, toks, HD), F32),
            jax.ShapeDtypeStruct((2, rows, HD), F32),
            jax.ShapeDtypeStruct((ne, cap, hidden), BF16),
        ],
        in_specs=[pl.BlockSpec(memory_space=pltpu.SMEM)] + [hbm] * 8,
        out_specs=[hbm] * 3,
        scratch_shapes=[
            pltpu.VMEM((heads * rows, HD), BF16),
            pltpu.VMEM((heads * rows, HD), BF16),
            pltpu.VMEM((rows, half), BF16),
            pltpu.VMEM((hidden, features), BF16),
            pltpu.VMEM((nx, nz, 2, toks, HD), BF16),
            pltpu.VMEM((nx + 1, max(blk, rows), heads * rows), F32),
            pltpu.VMEM((nx + 1, max(blk, rows), heads * rows), F32),
            pltpu.VMEM((3, 8, heads * rows), F32),
            pltpu.VMEM((2, 128, heads * rows), BF16),
            pltpu.VMEM((2, 128, heads * rows), BF16),
            pltpu.VMEM((nx - 1, 2, 2, blk // 2, HD), BF16),
            pltpu.VMEM((nx - 1, 2, 2, blk // 2, HD), BF16),
            pltpu.VMEM((2, 2, blk // 2, HD), F32),
            pltpu.VMEM((2, nz // 2, 2, toks, HD), BF16),
            pltpu.VMEM((nz, 2, toks, HD), BF16),
            pltpu.VMEM((ne, cap, half), BF16),
            pltpu.VMEM((2, ne, cap, half), BF16),
            pltpu.VMEM((2, rows, HD), F32),
            pltpu.VMEM((2, toks, HD), F32),
            pltpu.VMEM((ne, cap, hidden), BF16),
            pltpu.VMEM((toks, 2, HD), BF16),
            pltpu.VMEM((rows, 2, HD), BF16),
            pltpu.VMEM((routes.shape[3], rows), jnp.int32),
            pltpu.VMEM((routes.shape[3], rows), F32),
            dma((11,)),
            dma((nz - 1,)),
            dma((nz,)),
            dma((nx - 1, nz)),
            dma((nx - 1,)),
            dma((ne - 1,)),
            dma((ne,)),
            dma((1,)),
            dma((1,)),
            dma((nx - 1, 2)),
            dma((nx - 1, 2)),
            dma((nz,)),
            dma((nz,)),
            pltpu.SemaphoreType.REGULAR,
        ],
        compiler_params=pltpu.CompilerParams(
            collective_id=0, has_side_effects=True, vmem_limit_bytes=60 << 20
        ),
        name="moe_attention_backward",
    )(
        lengths,
        prompt_kv[0],
        resp_kv[0, 0],
        routes[0, 0].T,
        gates[0, 0].T,
        queries[0, 0],
        out_grad[0, 0],
        grads[0, 0],
        down_weight[0],
    )
    placed = pl.pallas_call(
        place,
        out_shape=[
            jax.ShapeDtypeStruct((toks, 2, HD), F32),
            jax.ShapeDtypeStruct((rows, 2, HD), F32),
            jax.ShapeDtypeStruct((ne, cap, hidden), BF16),
        ],
        in_specs=[vmem] * 3,
        out_specs=[vmem] * 3,
        compiler_params=pltpu.CompilerParams(vmem_limit_bytes=60 << 20),
        name="place_outputs",
    )(*out)
    return (placed[0][None], placed[1][None, None], placed[2][None, :, None])


def solution(mesh):
    nx = 4 if mesh.shape["seq"] == 32 else 2
    placed = (
        P("expert", "seq", None, "mp"),
        P("expert", "seq", None, "mp"),
        P("expert", "seq", None, "mp"),
        P("expert", "seq", None, None, "mp"),
        P("expert", "seq"),
        P("expert", "seq", None, None),
        P("expert", "seq", None, None),
        P("expert", "seq", None, None),
        P("expert", "mp", None),
    )
    return jax.shard_map(
        functools.partial(local, nx),
        mesh=mesh,
        in_specs=placed,
        out_specs=(
            P("expert", "seq", None, "mp"),
            P("expert", "seq", None, None, "mp"),
            P("seq", None, "expert", None, "mp"),
        ),
        check_vma=False,
    )
```

```python
import functools
import math

import jax
import jax.numpy as jnp
from jax import lax
from jax.experimental import pallas as pl
from jax.experimental.pallas import tpu as pltpu
from jax.sharding import PartitionSpec as P

HD = 128
SCALE = HD**-0.5
SCALE2 = SCALE * math.log2(math.e)
MESH = pl.DeviceIdType.MESH
F32 = jnp.float32
BF16 = jnp.bfloat16
NT = (((1,), (1,)), ((), ()))
NN = (((1,), (0,)), ((), ()))
TILE = 512


def kernel(
    nx,
    nz,
    len_ref,
    pkv_hbm,
    rkv_hbm,
    routes_hbm,
    gates_hbm,
    q_hbm,
    g_hbm,
    tok_hbm,
    w_hbm,
    pout,
    rout,
    eout,
    q,
    g,
    tok,
    w,
    gath,
    num,
    prob,
    stat,
    low_a,
    low_g,
    part1,
    recv1,
    own_sum,
    part2,
    recv2,
    rows_out,
    rows_in,
    own_grad,
    own_prompt,
    hid,
    pkv_ref,
    rkv_ref,
    routes_ref,
    gates_ref,
    local_sem,
    zs,
    zr,
    xs,
    xr,
    es,
    er,
    cs,
    cr,
    s1,
    r1,
    s2,
    r2,
    ready,
):
    seq = lax.axis_index("seq")
    me_e = lax.axis_index("expert")
    me_c = lax.axis_index("mp")
    me_x, me_z = seq // nz, seq % nz
    ne = rows_out.shape[0]
    cap = rows_out.shape[1]
    half = rows_out.shape[2]
    rows_all = q.shape[0]
    heads = rows_all // 128
    toks = gath.shape[3]
    blk = nz * toks

    def at_x(o):
        return {"seq": (me_x + o) % nx * nz + me_z}

    def at_z(o):
        return {"seq": me_x * nz + (me_z + o) % nz}

    ny = ne // 2
    me_h, me_y = me_e // ny, me_e % ny

    def at_y(o):
        return me_h * ny + (me_y + o) % ny

    def far(o):
        return (1 - me_h) * ny + (me_y + o) % ny

    sibling = {"mp": 1 - me_c}

    barrier = pltpu.get_barrier_semaphore()
    peers = [at_x(o) for o in range(1, nx)] + [at_z(o) for o in range(1, nz)]
    peers += [{"expert": at_y(o)} for o in range(1, ny)] + [sibling]

    @pl.when(me_h == 0)
    def _():
        for o in range(ny):
            pl.semaphore_signal(barrier, inc=1, device_id={"expert": far(o)}, device_id_type=MESH)

    for peer in peers:
        pl.semaphore_signal(barrier, inc=1, device_id=peer, device_id_type=MESH)

    small = [
        pltpu.make_async_copy(src, dst, local_sem.at[7 + k])
        for k, (src, dst) in enumerate(
            [(pkv_hbm, pkv_ref), (routes_hbm, routes_ref), (gates_hbm, gates_ref), (rkv_hbm, rkv_ref)]
        )
    ]
    for copy in small:
        copy.start()
    tok_copy = pltpu.make_async_copy(
        tok_hbm.at[:, pl.ds(pl.multiple_of(me_c * half, half), half)], tok, local_sem.at[2]
    )
    tok_copy.start()
    for h in range(heads):
        cols = slice(h * HD, (h + 1) * HD)
        pltpu.make_async_copy(q_hbm.at[:, cols], q.at[h * 128 : (h + 1) * 128], local_sem.at[0]).start()
        pltpu.make_async_copy(g_hbm.at[:, cols], g.at[h * 128 : (h + 1) * 128], local_sem.at[1]).start()
    w_copy = pltpu.make_async_copy(w_hbm, w, local_sem.at[3])
    w_copy.start()
    small[0].wait()
    gath[me_x, me_z, 0] = pkv_ref[:, 0, :]
    gath[me_x, me_z, 1] = pkv_ref[:, 1, :]
    pl.semaphore_wait(barrier, len(peers) + me_h * ny)

    @pl.when(me_h == 1)
    def _():
        for o in range(ny):
            pl.semaphore_signal(ready, inc=1, device_id={"expert": far(o)}, device_id_type=MESH)


    sends = []

    def remote(src, dst, send_sem, recv_sem, peer):
        copy = pltpu.make_async_remote_copy(
            src_ref=src,
            dst_ref=dst,
            send_sem=send_sem,
            recv_sem=recv_sem,
            device_id=peer,
            device_id_type=MESH,
        )
        copy.start()
        sends.append(copy)

    z_order = sorted(range(1, nz), key=lambda o: min(o, nz - o))
    own_block = gath.at[me_x, me_z]
    for o in reversed(z_order):
        remote(own_block, own_block, zs.at[o - 1], zr.at[me_z], at_z(o))

    def forward(k, zb):
        block = gath.at[me_x, zb]
        for o in range(1, nx):
            remote(block, block, xs.at[o - 1, k], xr.at[o - 1], at_x(o))

    forward(0, me_z)

    length = len_ref[0, 0]
    lane = lax.broadcasted_iota(jnp.int32, (1, 128), 1)
    small[1].wait()
    small[2].wait()
    route_t = routes_ref[...].astype(F32)
    gate_t = gates_ref[...]
    valid = (lane < length).astype(F32)
    named, weight = [], []
    for e in range(ne):
        hit = route_t == float(e)
        named.append(jnp.max(hit.astype(F32), 0, keepdims=True))
        weight.append(jnp.sum(jnp.where(hit, gate_t, 0.0), 0, keepdims=True) * valid)
    named_all = jnp.concatenate(named, 0)
    upper = (
        lax.broadcasted_iota(jnp.int32, (128, 128), 0) <= lax.broadcasted_iota(jnp.int32, (128, 128), 1)
    ).astype(BF16)
    slot = lax.dot_general(named_all.astype(BF16), upper, NN, preferred_element_type=F32) - 1.0
    slot_id = lax.broadcasted_iota(jnp.int32, (cap, 128), 0).astype(F32)
    select, slot_gate = [], []
    for e in range(ne):
        chosen = jnp.where(slot[e : e + 1] == slot_id, named[e], 0.0)
        select.append(chosen)
        slot_gate.append(jnp.sum(chosen * weight[e], 1, keepdims=True))
    select = jnp.concatenate(select, 0).astype(BF16)
    slot_gate = jnp.concatenate(slot_gate, 0)
    tok_copy.wait()
    picked = lax.dot_general(select, tok[...], NN, preferred_element_type=F32)
    rows_out[...] = (picked * slot_gate).astype(BF16).reshape(ne, cap, half)

    def routed(there, k):
        return pltpu.make_async_remote_copy(
            src_ref=rows_out.at[there],
            dst_ref=rows_in.at[me_c, me_e],
            send_sem=es.at[k],
            recv_sem=er.at[me_e],
            device_id={"expert": there},
            device_id_type=MESH,
        )

    near_rows = [routed(at_y(o), o - 1) for o in range(1, ny)]
    far_rows = [routed(far(o), ny - 1 + o) for o in range(ny)]

    @pl.when(me_h == 1)
    def _():
        for copy in far_rows:
            copy.start()

    for copy in near_rows:
        copy.start()
    rows_in[me_c, me_e] = rows_out[me_e]

    pltpu.make_async_copy(q, q, local_sem.at[0]).wait()
    pltpu.make_async_copy(g, g, local_sem.at[1]).wait()
    row_at = lax.broadcasted_iota(jnp.int32, (128, HD), 0)
    for h in range(heads):
        part = g[h * 128 : (h + 1) * 128, :]
        g[h * 128 : (h + 1) * 128, :] = jnp.where(row_at < length, part.astype(F32), 0.0).astype(BF16)

    def forward_block(b, keys, values, causal):
        n = keys.shape[0]
        for t in range(rows_all // TILE):
            rows = slice(t * TILE, (t + 1) * TILE)
            score = lax.dot_general(keys, q[rows, :], NT, preferred_element_type=F32)
            if causal:
                key_at = lax.broadcasted_iota(jnp.int32, (n, TILE), 0)
                query_at = lax.broadcasted_iota(jnp.int32, (n, TILE), 1) % 128
                score = jnp.where(key_at <= query_at, score, -jnp.inf)
            top = jnp.max(score, 0, keepdims=True)
            exps = jnp.exp2((score - top) * SCALE2)
            probs = lax.dot_general(values, g[rows, :], NT, preferred_element_type=F32)
            stat[0, b : b + 1, rows] = top
            stat[1, b : b + 1, rows] = jnp.sum(exps, 0, keepdims=True)
            stat[2, b : b + 1, rows] = jnp.sum(exps * probs, 0, keepdims=True)
            num[b, 0:n, rows] = exps
            prob[b, 0:n, rows] = probs

    own_b = nx
    small[3].wait()
    forward_block(own_b, rkv_ref[:, 0, :], rkv_ref[:, 1, :], True)

    for k, o in enumerate(z_order):
        zb = (me_z + o) % nz
        block = gath.at[me_x, zb]
        pltpu.make_async_copy(block, block, zr.at[zb]).wait()
        forward(k + 1, zb)

    x_order = sorted(range(1, nx), key=lambda o: min(o, nx - o))
    for b, o in enumerate([0] + x_order):
        xb = (me_x + nx - o) % nx
        if o:
            came = gath.at[xb]
            pltpu.make_async_copy(came, came, xr.at[o - 1]).wait()
        forward_block(
            b, gath[xb, :, 0].reshape(blk, HD), gath[xb, :, 1].reshape(blk, HD), False
        )
        if b == 0:
            @pl.when(me_h == 0)
            def _():
                pl.semaphore_wait(ready, ny)
                for copy in far_rows:
                    copy.start()

    nb = nx + 1
    top = stat[0, 0:nb, :]
    factor = jnp.exp2((top - jnp.max(top, 0, keepdims=True)) * SCALE2)
    inverse = 1.0 / jnp.sum(stat[1, 0:nb, :] * factor, 0, keepdims=True)
    delta = jnp.sum(stat[2, 0:nb, :] * factor, 0, keepdims=True) * inverse
    stat[0, 0:nb, :] = factor * inverse
    stat[1, 0:1, :] = delta

    def backward_block(b, keys, n, at):
        for t in range(rows_all // 256):
            rows = slice(t * 256, (t + 1) * 256)
            attention = num[b, keys, rows] * stat[0, b : b + 1, rows]
            grad = attention * ((prob[b, keys, rows] - stat[1, 0:1, rows]) * SCALE)
            low_a[at, 0:n, rows] = attention.astype(BF16)
            low_g[at, 0:n, rows] = grad.astype(BF16)
        grad_v = lax.dot_general(low_a[at, 0:n, :], g[...], NN, preferred_element_type=F32)
        grad_k = lax.dot_general(low_g[at, 0:n, :], q[...], NN, preferred_element_type=F32)
        return grad_k, grad_v

    hz = nz // 2
    sub = hz * toks
    my_half, my_at = me_z // hz, me_z % hz
    halves = [1 - my_half, my_half]
    for step in range(2):
        keys = pl.ds(pl.multiple_of(halves[step] * sub, sub), sub)
        for b, o in reversed(list(enumerate([0] + x_order))):
            grad_k, grad_v = backward_block(b, keys, sub, b % 2)
            if o:
                part1[b - 1, step, 0] = grad_k.astype(BF16)
                part1[b - 1, step, 1] = grad_v.astype(BF16)
                remote(
                    part1.at[b - 1, step],
                    recv1.at[o - 1, step],
                    s1.at[o - 1, step],
                    r1.at[o - 1, step],
                    at_x(nx - o),
                )
            else:
                own_sum[step, 0] = grad_k
                own_sum[step, 1] = grad_v

    grad_k, grad_v = backward_block(own_b, slice(0, 128), 128, 1)
    own_grad[0] = grad_k
    own_grad[1] = grad_v
    own_out = pltpu.make_async_copy(own_grad, rout, local_sem.at[4])
    own_out.start()

    def swap(h, k, sources):
        for there in sources:
            came = rows_in.at[me_c, there]
            pltpu.make_async_copy(came, came, er.at[there]).wait()
        part = rows_in.at[me_c, pl.ds(pl.multiple_of(h * ny, ny), ny)]
        remote(part, part, cs.at[k], cr.at[k], sibling)

    sent = len(sends)
    swap(me_h, 0, [at_y(o) for o in range(1, ny)])

    for step in range(2):
        for o in range(1, nx):
            came = recv1.at[o - 1, step]
            pltpu.make_async_copy(came, came, r1.at[o - 1, step]).wait()
        for j in range(hz):
            keys = slice(j * toks, (j + 1) * toks)
            for kv in range(2):
                total = own_sum[step, kv, keys, :]
                for o in range(1, nx):
                    total = total + recv1[o - 1, step, kv, keys, :].astype(F32)
                own_sum[step, kv, keys, :] = total
                part2[step, j, kv] = total.astype(BF16)
        for o in range(step, hz):
            j = (my_at + o) % hz
            remote(
                part2.at[step, j],
                recv2.at[me_z],
                s2.at[step * hz + o],
                r2.at[me_z],
                {"seq": me_x * nz + halves[step] * hz + j},
            )

    for copy in sends[:sent]:
        copy.wait_send()
    swap(1 - me_h, 1, [far(o) for o in range(ny)])

    w_copy.wait()
    for k, h in enumerate([me_h, 1 - me_h]):
        other = rows_in.at[1 - me_c, pl.ds(pl.multiple_of(h * ny, ny), ny)]
        pltpu.make_async_copy(other, other, cr.at[k]).wait()
    hidden = lax.dot_general(
        rows_in[0].reshape(ne * cap, half), w[:, 0:half], NT, preferred_element_type=F32
    )
    hidden = hidden + lax.dot_general(
        rows_in[1].reshape(ne * cap, half), w[:, half : 2 * half], NT, preferred_element_type=F32
    )
    hid[...] = hidden.astype(BF16).reshape(hid.shape)
    hid_out = pltpu.make_async_copy(hid, eout, local_sem.at[5])
    hid_out.start()

    mine = pl.ds(pl.multiple_of(my_at * toks, toks), toks)
    total_k, total_v = own_sum[1, 0, mine, :], own_sum[1, 1, mine, :]
    for o in z_order:
        zb = (me_z + o) % nz
        came = recv2.at[zb]
        pltpu.make_async_copy(came, came, r2.at[zb]).wait()
        total_k = total_k + recv2[zb, 0].astype(F32)
        total_v = total_v + recv2[zb, 1].astype(F32)
    own_prompt[0] = total_k
    own_prompt[1] = total_v
    prompt_out = pltpu.make_async_copy(own_prompt, pout, local_sem.at[6])
    prompt_out.start()
    own_out.wait()
    hid_out.wait()
    prompt_out.wait()
    for copy in sends[sent:] + near_rows + far_rows:
        copy.wait_send()


def place(pin, rin, ein, pout, rout, eout):
    for kv in range(2):
        pout[:, kv, :] = pin[kv]
        rout[:, kv, :] = rin[kv]
    eout[...] = ein[...]


def local(nx, queries, out_grad, prompt_kv, resp_kv, lengths, grads, routes, gates, down_weight):
    ne = lax.axis_size("expert")
    toks = prompt_kv.shape[1]
    rows = queries.shape[2]
    width = queries.shape[3]
    heads = width // HD
    nz = lax.axis_size("seq") // nx
    features = grads.shape[3]
    half = features // 2
    hidden = down_weight.shape[1]
    cap = rows // 8
    blk = nz * toks
    vmem = pl.BlockSpec(memory_space=pltpu.VMEM)
    hbm = pl.BlockSpec(memory_space=pl.ANY)
    dma = pltpu.SemaphoreType.DMA
    out = pl.pallas_call(
        functools.partial(kernel, nx, nz),
        out_shape=[
            jax.ShapeDtypeStruct((2, toks, HD), F32),
            jax.ShapeDtypeStruct((2, rows, HD), F32),
            jax.ShapeDtypeStruct((ne, cap, hidden), BF16),
        ],
        in_specs=[pl.BlockSpec(memory_space=pltpu.SMEM)] + [hbm] * 8,
        out_specs=[hbm] * 3,
        scratch_shapes=[
            pltpu.VMEM((heads * rows, HD), BF16),
            pltpu.VMEM((heads * rows, HD), BF16),
            pltpu.VMEM((rows, half), BF16),
            pltpu.VMEM((hidden, features), BF16),
            pltpu.VMEM((nx, nz, 2, toks, HD), BF16),
            pltpu.VMEM((nx + 1, max(blk, rows), heads * rows), F32),
            pltpu.VMEM((nx + 1, max(blk, rows), heads * rows), F32),
            pltpu.VMEM((3, 8, heads * rows), F32),
            pltpu.VMEM((2, 128, heads * rows), BF16),
            pltpu.VMEM((2, 128, heads * rows), BF16),
            pltpu.VMEM((nx - 1, 2, 2, blk // 2, HD), BF16),
            pltpu.VMEM((nx - 1, 2, 2, blk // 2, HD), BF16),
            pltpu.VMEM((2, 2, blk // 2, HD), F32),
            pltpu.VMEM((2, nz // 2, 2, toks, HD), BF16),
            pltpu.VMEM((nz, 2, toks, HD), BF16),
            pltpu.VMEM((ne, cap, half), BF16),
            pltpu.VMEM((2, ne, cap, half), BF16),
            pltpu.VMEM((2, rows, HD), F32),
            pltpu.VMEM((2, toks, HD), F32),
            pltpu.VMEM((ne, cap, hidden), BF16),
            pltpu.VMEM((toks, 2, HD), BF16),
            pltpu.VMEM((rows, 2, HD), BF16),
            pltpu.VMEM((routes.shape[3], rows), jnp.int32),
            pltpu.VMEM((routes.shape[3], rows), F32),
            dma((11,)),
            dma((nz - 1,)),
            dma((nz,)),
            dma((nx - 1, nz)),
            dma((nx - 1,)),
            dma((ne - 1,)),
            dma((ne,)),
            dma((2,)),
            dma((2,)),
            dma((nx - 1, 2)),
            dma((nx - 1, 2)),
            dma((nz,)),
            dma((nz,)),
            pltpu.SemaphoreType.REGULAR,
        ],
        compiler_params=pltpu.CompilerParams(
            collective_id=0, has_side_effects=True, vmem_limit_bytes=60 << 20
        ),
        name="moe_attention_backward",
    )(
        lengths,
        prompt_kv[0],
        resp_kv[0, 0],
        routes[0, 0].T,
        gates[0, 0].T,
        queries[0, 0],
        out_grad[0, 0],
        grads[0, 0],
        down_weight[0],
    )
    placed = pl.pallas_call(
        place,
        out_shape=[
            jax.ShapeDtypeStruct((toks, 2, HD), F32),
            jax.ShapeDtypeStruct((rows, 2, HD), F32),
            jax.ShapeDtypeStruct((ne, cap, hidden), BF16),
        ],
        in_specs=[vmem] * 3,
        out_specs=[vmem] * 3,
        compiler_params=pltpu.CompilerParams(vmem_limit_bytes=60 << 20),
        name="place_outputs",
    )(*out)
    return (placed[0][None], placed[1][None, None], placed[2][None, :, None])


def solution(mesh):
    nx = 4 if mesh.shape["seq"] == 32 else 2
    placed = (
        P("expert", "seq", None, "mp"),
        P("expert", "seq", None, "mp"),
        P("expert", "seq", None, "mp"),
        P("expert", "seq", None, None, "mp"),
        P("expert", "seq"),
        P("expert", "seq", None, None),
        P("expert", "seq", None, None),
        P("expert", "seq", None, None),
        P("expert", "mp", None),
    )
    return jax.shard_map(
        functools.partial(local, nx),
        mesh=mesh,
        in_specs=placed,
        out_specs=(
            P("expert", "seq", None, "mp"),
            P("expert", "seq", None, None, "mp"),
            P("seq", None, "expert", None, "mp"),
        ),
        check_vma=False,
    )
```

```python
import functools
import math

import jax
import jax.numpy as jnp
from jax import lax
from jax.experimental import pallas as pl
from jax.experimental.pallas import tpu as pltpu
from jax.sharding import PartitionSpec as P

HD = 128
SCALE = HD**-0.5
SCALE2 = SCALE * math.log2(math.e)
MESH = pl.DeviceIdType.MESH
F32 = jnp.float32
BF16 = jnp.bfloat16
NT = (((1,), (1,)), ((), ()))
NN = (((1,), (0,)), ((), ()))
TILE = 512


def kernel(
    nx,
    nz,
    len_ref,
    pkv_hbm,
    rkv_hbm,
    routes_hbm,
    gates_hbm,
    q_hbm,
    g_hbm,
    tok_hbm,
    w_hbm,
    pout,
    rout,
    eout,
    q,
    g,
    tok,
    w,
    gath,
    num,
    prob,
    stat,
    low_a,
    low_g,
    part1,
    recv1,
    own_sum,
    part2,
    recv2,
    rows_out,
    rows_in,
    own_grad,
    own_prompt,
    hid,
    pkv_ref,
    rkv_ref,
    routes_ref,
    gates_ref,
    local_sem,
    zs,
    zr,
    xs,
    xr,
    es,
    er,
    cs,
    cr,
    s1,
    r1,
    s2,
    r2,
    ready,
):
    seq = lax.axis_index("seq")
    me_e = lax.axis_index("expert")
    me_c = lax.axis_index("mp")
    me_x, me_z = seq // nz, seq % nz
    ne = rows_out.shape[0]
    cap = rows_out.shape[1]
    half = rows_out.shape[2]
    rows_all = q.shape[0]
    heads = rows_all // 128
    toks = gath.shape[3]
    blk = nz * toks

    def at_x(o):
        return {"seq": (me_x + o) % nx * nz + me_z}

    def at_z(o):
        return {"seq": me_x * nz + (me_z + o) % nz}

    ny = ne // 2
    me_h, me_y = me_e // ny, me_e % ny

    def at_y(o):
        return me_h * ny + (me_y + o) % ny

    def far(o):
        return (1 - me_h) * ny + (me_y + o) % ny

    sibling = {"mp": 1 - me_c}

    barrier = pltpu.get_barrier_semaphore()
    peers = [at_x(o) for o in range(1, nx)] + [at_z(o) for o in range(1, nz)]
    peers += [{"expert": at_y(o)} for o in range(1, ny)] + [sibling]

    @pl.when(me_h == 0)
    def _():
        for o in range(ny):
            pl.semaphore_signal(barrier, inc=1, device_id={"expert": far(o)}, device_id_type=MESH)

    for peer in peers:
        pl.semaphore_signal(barrier, inc=1, device_id=peer, device_id_type=MESH)

    small = [
        pltpu.make_async_copy(src, dst, local_sem.at[7 + k])
        for k, (src, dst) in enumerate(
            [(pkv_hbm, pkv_ref), (routes_hbm, routes_ref), (gates_hbm, gates_ref), (rkv_hbm, rkv_ref)]
        )
    ]
    for copy in small:
        copy.start()
    tok_copy = pltpu.make_async_copy(
        tok_hbm.at[:, pl.ds(pl.multiple_of(me_c * half, half), half)], tok, local_sem.at[2]
    )
    tok_copy.start()
    for h in range(heads):
        cols = slice(h * HD, (h + 1) * HD)
        pltpu.make_async_copy(q_hbm.at[:, cols], q.at[h * 128 : (h + 1) * 128], local_sem.at[0]).start()
        pltpu.make_async_copy(g_hbm.at[:, cols], g.at[h * 128 : (h + 1) * 128], local_sem.at[1]).start()
    w_copy = pltpu.make_async_copy(w_hbm, w, local_sem.at[3])
    w_copy.start()
    small[0].wait()
    gath[me_x, me_z, 0] = pkv_ref[:, 0, :]
    gath[me_x, me_z, 1] = pkv_ref[:, 1, :]
    pl.semaphore_wait(barrier, len(peers) + me_h * ny)

    @pl.when(me_h == 1)
    def _():
        for o in range(ny):
            pl.semaphore_signal(ready, inc=1, device_id={"expert": far(o)}, device_id_type=MESH)


    sends = []

    def remote(src, dst, send_sem, recv_sem, peer):
        copy = pltpu.make_async_remote_copy(
            src_ref=src,
            dst_ref=dst,
            send_sem=send_sem,
            recv_sem=recv_sem,
            device_id=peer,
            device_id_type=MESH,
        )
        copy.start()
        sends.append(copy)

    z_order = sorted(range(1, nz), key=lambda o: min(o, nz - o))
    own_block = gath.at[me_x, me_z]
    for o in reversed(z_order):
        remote(own_block, own_block, zs.at[o - 1], zr.at[me_z], at_z(o))

    def forward(k, zb):
        block = gath.at[me_x, zb]
        for o in range(1, nx):
            remote(block, block, xs.at[o - 1, k], xr.at[o - 1], at_x(o))

    forward(0, me_z)

    length = len_ref[0, 0]
    lane = lax.broadcasted_iota(jnp.int32, (1, 128), 1)
    small[1].wait()
    small[2].wait()
    route_t = routes_ref[...].astype(F32)
    gate_t = gates_ref[...]
    valid = (lane < length).astype(F32)
    named, weight = [], []
    for e in range(ne):
        hit = route_t == float(e)
        named.append(jnp.max(hit.astype(F32), 0, keepdims=True))
        weight.append(jnp.sum(jnp.where(hit, gate_t, 0.0), 0, keepdims=True) * valid)
    named_all = jnp.concatenate(named, 0)
    upper = (
        lax.broadcasted_iota(jnp.int32, (128, 128), 0) <= lax.broadcasted_iota(jnp.int32, (128, 128), 1)
    ).astype(BF16)
    slot = lax.dot_general(named_all.astype(BF16), upper, NN, preferred_element_type=F32) - 1.0
    slot_id = lax.broadcasted_iota(jnp.int32, (cap, 128), 0).astype(F32)
    select, slot_gate = [], []
    for e in range(ne):
        chosen = jnp.where(slot[e : e + 1] == slot_id, named[e], 0.0)
        select.append(chosen)
        slot_gate.append(jnp.sum(chosen * weight[e], 1, keepdims=True))
    select = jnp.concatenate(select, 0).astype(BF16)
    slot_gate = jnp.concatenate(slot_gate, 0)
    tok_copy.wait()
    picked = lax.dot_general(select, tok[...], NN, preferred_element_type=F32)
    rows_out[...] = (picked * slot_gate).astype(BF16).reshape(ne, cap, half)

    def routed(there, k):
        return pltpu.make_async_remote_copy(
            src_ref=rows_out.at[there],
            dst_ref=rows_in.at[me_c, me_e],
            send_sem=es.at[k],
            recv_sem=er.at[me_e],
            device_id={"expert": there},
            device_id_type=MESH,
        )

    near_rows = [routed(at_y(o), o - 1) for o in range(1, ny)]
    far_rows = [routed(far(o), ny - 1 + o) for o in range(ny)]

    rows_in[me_c, me_e] = rows_out[me_e]

    pltpu.make_async_copy(q, q, local_sem.at[0]).wait()
    pltpu.make_async_copy(g, g, local_sem.at[1]).wait()
    row_at = lax.broadcasted_iota(jnp.int32, (128, HD), 0)
    for h in range(heads):
        part = g[h * 128 : (h + 1) * 128, :]
        g[h * 128 : (h + 1) * 128, :] = jnp.where(row_at < length, part.astype(F32), 0.0).astype(BF16)

    def forward_block(b, keys, values, causal):
        n = keys.shape[0]
        for t in range(rows_all // TILE):
            rows = slice(t * TILE, (t + 1) * TILE)
            score = lax.dot_general(keys, q[rows, :], NT, preferred_element_type=F32)
            if causal:
                key_at = lax.broadcasted_iota(jnp.int32, (n, TILE), 0)
                query_at = lax.broadcasted_iota(jnp.int32, (n, TILE), 1) % 128
                score = jnp.where(key_at <= query_at, score, -jnp.inf)
            top = jnp.max(score, 0, keepdims=True)
            exps = jnp.exp2((score - top) * SCALE2)
            probs = lax.dot_general(values, g[rows, :], NT, preferred_element_type=F32)
            stat[0, b : b + 1, rows] = top
            stat[1, b : b + 1, rows] = jnp.sum(exps, 0, keepdims=True)
            stat[2, b : b + 1, rows] = jnp.sum(exps * probs, 0, keepdims=True)
            num[b, 0:n, rows] = exps
            prob[b, 0:n, rows] = probs

    own_b = nx
    small[3].wait()
    forward_block(own_b, rkv_ref[:, 0, :], rkv_ref[:, 1, :], True)

    for k, o in enumerate(z_order):
        zb = (me_z + o) % nz
        block = gath.at[me_x, zb]
        pltpu.make_async_copy(block, block, zr.at[zb]).wait()
        forward(k + 1, zb)
        if k < ny:
            pl.when(me_h == 1)(far_rows[k].start)

    for copy in near_rows:
        copy.start()

    x_order = sorted(range(1, nx), key=lambda o: min(o, nx - o))
    for b, o in enumerate([0] + x_order):
        xb = (me_x + nx - o) % nx
        if o:
            came = gath.at[xb]
            pltpu.make_async_copy(came, came, xr.at[o - 1]).wait()
        forward_block(
            b, gath[xb, :, 0].reshape(blk, HD), gath[xb, :, 1].reshape(blk, HD), False
        )
        if b == 0:
            @pl.when(me_h == 0)
            def _():
                pl.semaphore_wait(ready, ny)
                for copy in far_rows:
                    copy.start()

    nb = nx + 1
    top = stat[0, 0:nb, :]
    factor = jnp.exp2((top - jnp.max(top, 0, keepdims=True)) * SCALE2)
    inverse = 1.0 / jnp.sum(stat[1, 0:nb, :] * factor, 0, keepdims=True)
    delta = jnp.sum(stat[2, 0:nb, :] * factor, 0, keepdims=True) * inverse
    stat[0, 0:nb, :] = factor * inverse
    stat[1, 0:1, :] = delta

    def backward_block(b, keys, n, at):
        for t in range(rows_all // 256):
            rows = slice(t * 256, (t + 1) * 256)
            attention = num[b, keys, rows] * stat[0, b : b + 1, rows]
            grad = attention * ((prob[b, keys, rows] - stat[1, 0:1, rows]) * SCALE)
            low_a[at, 0:n, rows] = attention.astype(BF16)
            low_g[at, 0:n, rows] = grad.astype(BF16)
        grad_v = lax.dot_general(low_a[at, 0:n, :], g[...], NN, preferred_element_type=F32)
        grad_k = lax.dot_general(low_g[at, 0:n, :], q[...], NN, preferred_element_type=F32)
        return grad_k, grad_v

    hz = nz // 2
    sub = hz * toks
    my_half, my_at = me_z // hz, me_z % hz
    halves = [1 - my_half, my_half]
    for step in range(2):
        keys = pl.ds(pl.multiple_of(halves[step] * sub, sub), sub)
        for b, o in reversed(list(enumerate([0] + x_order))):
            grad_k, grad_v = backward_block(b, keys, sub, b % 2)
            if o:
                part1[b - 1, step, 0] = grad_k.astype(BF16)
                part1[b - 1, step, 1] = grad_v.astype(BF16)
                remote(
                    part1.at[b - 1, step],
                    recv1.at[o - 1, step],
                    s1.at[o - 1, step],
                    r1.at[o - 1, step],
                    at_x(nx - o),
                )
            else:
                own_sum[step, 0] = grad_k
                own_sum[step, 1] = grad_v

    grad_k, grad_v = backward_block(own_b, slice(0, 128), 128, 1)
    own_grad[0] = grad_k
    own_grad[1] = grad_v
    own_out = pltpu.make_async_copy(own_grad, rout, local_sem.at[4])
    own_out.start()

    def swap(h, k, sources):
        for there in sources:
            came = rows_in.at[me_c, there]
            pltpu.make_async_copy(came, came, er.at[there]).wait()
        part = rows_in.at[me_c, pl.ds(pl.multiple_of(h * ny, ny), ny)]
        remote(part, part, cs.at[k], cr.at[k], sibling)

    sent = len(sends)
    swap(me_h, 0, [at_y(o) for o in range(1, ny)])

    for step in range(2):
        for o in range(1, nx):
            came = recv1.at[o - 1, step]
            pltpu.make_async_copy(came, came, r1.at[o - 1, step]).wait()
        for j in range(hz):
            keys = slice(j * toks, (j + 1) * toks)
            for kv in range(2):
                total = own_sum[step, kv, keys, :]
                for o in range(1, nx):
                    total = total + recv1[o - 1, step, kv, keys, :].astype(F32)
                own_sum[step, kv, keys, :] = total
                part2[step, j, kv] = total.astype(BF16)
        for o in range(step, hz):
            j = (my_at + o) % hz
            remote(
                part2.at[step, j],
                recv2.at[me_z],
                s2.at[step * hz + o],
                r2.at[me_z],
                {"seq": me_x * nz + halves[step] * hz + j},
            )

    for copy in sends[:sent]:
        copy.wait_send()
    swap(1 - me_h, 1, [far(o) for o in range(ny)])

    w_copy.wait()
    for k, h in enumerate([me_h, 1 - me_h]):
        other = rows_in.at[1 - me_c, pl.ds(pl.multiple_of(h * ny, ny), ny)]
        pltpu.make_async_copy(other, other, cr.at[k]).wait()
    hidden = lax.dot_general(
        rows_in[0].reshape(ne * cap, half), w[:, 0:half], NT, preferred_element_type=F32
    )
    hidden = hidden + lax.dot_general(
        rows_in[1].reshape(ne * cap, half), w[:, half : 2 * half], NT, preferred_element_type=F32
    )
    hid[...] = hidden.astype(BF16).reshape(hid.shape)
    hid_out = pltpu.make_async_copy(hid, eout, local_sem.at[5])
    hid_out.start()

    mine = pl.ds(pl.multiple_of(my_at * toks, toks), toks)
    total_k, total_v = own_sum[1, 0, mine, :], own_sum[1, 1, mine, :]
    for o in z_order:
        zb = (me_z + o) % nz
        came = recv2.at[zb]
        pltpu.make_async_copy(came, came, r2.at[zb]).wait()
        total_k = total_k + recv2[zb, 0].astype(F32)
        total_v = total_v + recv2[zb, 1].astype(F32)
    own_prompt[0] = total_k
    own_prompt[1] = total_v
    prompt_out = pltpu.make_async_copy(own_prompt, pout, local_sem.at[6])
    prompt_out.start()
    own_out.wait()
    hid_out.wait()
    prompt_out.wait()
    for copy in sends[sent:] + near_rows + far_rows:
        copy.wait_send()


def place(pin, rin, ein, pout, rout, eout):
    for kv in range(2):
        pout[:, kv, :] = pin[kv]
        rout[:, kv, :] = rin[kv]
    eout[...] = ein[...]


def local(nx, queries, out_grad, prompt_kv, resp_kv, lengths, grads, routes, gates, down_weight):
    ne = lax.axis_size("expert")
    toks = prompt_kv.shape[1]
    rows = queries.shape[2]
    width = queries.shape[3]
    heads = width // HD
    nz = lax.axis_size("seq") // nx
    features = grads.shape[3]
    half = features // 2
    hidden = down_weight.shape[1]
    cap = rows // 8
    blk = nz * toks
    vmem = pl.BlockSpec(memory_space=pltpu.VMEM)
    hbm = pl.BlockSpec(memory_space=pl.ANY)
    dma = pltpu.SemaphoreType.DMA
    out = pl.pallas_call(
        functools.partial(kernel, nx, nz),
        out_shape=[
            jax.ShapeDtypeStruct((2, toks, HD), F32),
            jax.ShapeDtypeStruct((2, rows, HD), F32),
            jax.ShapeDtypeStruct((ne, cap, hidden), BF16),
        ],
        in_specs=[pl.BlockSpec(memory_space=pltpu.SMEM)] + [hbm] * 8,
        out_specs=[hbm] * 3,
        scratch_shapes=[
            pltpu.VMEM((heads * rows, HD), BF16),
            pltpu.VMEM((heads * rows, HD), BF16),
            pltpu.VMEM((rows, half), BF16),
            pltpu.VMEM((hidden, features), BF16),
            pltpu.VMEM((nx, nz, 2, toks, HD), BF16),
            pltpu.VMEM((nx + 1, max(blk, rows), heads * rows), F32),
            pltpu.VMEM((nx + 1, max(blk, rows), heads * rows), F32),
            pltpu.VMEM((3, 8, heads * rows), F32),
            pltpu.VMEM((2, 128, heads * rows), BF16),
            pltpu.VMEM((2, 128, heads * rows), BF16),
            pltpu.VMEM((nx - 1, 2, 2, blk // 2, HD), BF16),
            pltpu.VMEM((nx - 1, 2, 2, blk // 2, HD), BF16),
            pltpu.VMEM((2, 2, blk // 2, HD), F32),
            pltpu.VMEM((2, nz // 2, 2, toks, HD), BF16),
            pltpu.VMEM((nz, 2, toks, HD), BF16),
            pltpu.VMEM((ne, cap, half), BF16),
            pltpu.VMEM((2, ne, cap, half), BF16),
            pltpu.VMEM((2, rows, HD), F32),
            pltpu.VMEM((2, toks, HD), F32),
            pltpu.VMEM((ne, cap, hidden), BF16),
            pltpu.VMEM((toks, 2, HD), BF16),
            pltpu.VMEM((rows, 2, HD), BF16),
            pltpu.VMEM((routes.shape[3], rows), jnp.int32),
            pltpu.VMEM((routes.shape[3], rows), F32),
            dma((11,)),
            dma((nz - 1,)),
            dma((nz,)),
            dma((nx - 1, nz)),
            dma((nx - 1,)),
            dma((ne - 1,)),
            dma((ne,)),
            dma((2,)),
            dma((2,)),
            dma((nx - 1, 2)),
            dma((nx - 1, 2)),
            dma((nz,)),
            dma((nz,)),
            pltpu.SemaphoreType.REGULAR,
        ],
        compiler_params=pltpu.CompilerParams(
            collective_id=0, has_side_effects=True, vmem_limit_bytes=60 << 20
        ),
        name="moe_attention_backward",
    )(
        lengths,
        prompt_kv[0],
        resp_kv[0, 0],
        routes[0, 0].T,
        gates[0, 0].T,
        queries[0, 0],
        out_grad[0, 0],
        grads[0, 0],
        down_weight[0],
    )
    placed = pl.pallas_call(
        place,
        out_shape=[
            jax.ShapeDtypeStruct((toks, 2, HD), F32),
            jax.ShapeDtypeStruct((rows, 2, HD), F32),
            jax.ShapeDtypeStruct((ne, cap, hidden), BF16),
        ],
        in_specs=[vmem] * 3,
        out_specs=[vmem] * 3,
        compiler_params=pltpu.CompilerParams(vmem_limit_bytes=60 << 20),
        name="place_outputs",
    )(*out)
    return (placed[0][None], placed[1][None, None], placed[2][None, :, None])


def solution(mesh):
    nx = 4 if mesh.shape["seq"] == 32 else 2
    placed = (
        P("expert", "seq", None, "mp"),
        P("expert", "seq", None, "mp"),
        P("expert", "seq", None, "mp"),
        P("expert", "seq", None, None, "mp"),
        P("expert", "seq"),
        P("expert", "seq", None, None),
        P("expert", "seq", None, None),
        P("expert", "seq", None, None),
        P("expert", "mp", None),
    )
    return jax.shard_map(
        functools.partial(local, nx),
        mesh=mesh,
        in_specs=placed,
        out_specs=(
            P("expert", "seq", None, "mp"),
            P("expert", "seq", None, None, "mp"),
            P("seq", None, "expert", None, "mp"),
        ),
        check_vma=False,
    )
```

```python
import functools
import math

import jax
import jax.numpy as jnp
from jax import lax
from jax.experimental import pallas as pl
from jax.experimental.pallas import tpu as pltpu
from jax.sharding import PartitionSpec as P

HD = 128
SCALE = HD**-0.5
SCALE2 = SCALE * math.log2(math.e)
MESH = pl.DeviceIdType.MESH
F32 = jnp.float32
BF16 = jnp.bfloat16
NT = (((1,), (1,)), ((), ()))
NN = (((1,), (0,)), ((), ()))
TILE = 512


def kernel(
    nx,
    nz,
    len_ref,
    pkv_hbm,
    rkv_hbm,
    routes_hbm,
    gates_hbm,
    q_hbm,
    g_hbm,
    tok_hbm,
    w_hbm,
    pout,
    rout,
    eout,
    q,
    g,
    tok,
    w,
    gath,
    num,
    prob,
    stat,
    low_a,
    low_g,
    part1,
    recv1,
    own_sum,
    part2,
    recv2,
    rows_out,
    rows_in,
    own_grad,
    own_prompt,
    hid,
    pkv_ref,
    rkv_ref,
    routes_ref,
    gates_ref,
    local_sem,
    zs,
    zr,
    xs,
    xr,
    es,
    er,
    cs,
    cr,
    s1,
    r1,
    s2,
    r2,
    ready,
):
    seq = lax.axis_index("seq")
    me_e = lax.axis_index("expert")
    me_c = lax.axis_index("mp")
    me_x, me_z = seq // nz, seq % nz
    ne = rows_out.shape[0]
    cap = rows_out.shape[1]
    half = rows_out.shape[2]
    rows_all = q.shape[0]
    heads = rows_all // 128
    toks = gath.shape[3]
    blk = nz * toks

    def at_x(o):
        return {"seq": (me_x + o) % nx * nz + me_z}

    def at_z(o):
        return {"seq": me_x * nz + (me_z + o) % nz}

    ny = ne // 2
    me_h, me_y = me_e // ny, me_e % ny

    def at_y(o):
        return me_h * ny + (me_y + o) % ny

    def far(o):
        return (1 - me_h) * ny + (me_y + o) % ny

    sibling = {"mp": 1 - me_c}

    barrier = pltpu.get_barrier_semaphore()
    peers = [at_x(o) for o in range(1, nx)] + [at_z(o) for o in range(1, nz)]
    peers += [{"expert": at_y(o)} for o in range(1, ny)] + [sibling]

    @pl.when(me_h == 0)
    def _():
        for o in range(ny):
            pl.semaphore_signal(barrier, inc=1, device_id={"expert": far(o)}, device_id_type=MESH)

    for peer in peers:
        pl.semaphore_signal(barrier, inc=1, device_id=peer, device_id_type=MESH)

    small = [
        pltpu.make_async_copy(src, dst, local_sem.at[7 + k])
        for k, (src, dst) in enumerate(
            [(pkv_hbm, pkv_ref), (routes_hbm, routes_ref), (gates_hbm, gates_ref), (rkv_hbm, rkv_ref)]
        )
    ]
    for copy in small:
        copy.start()
    tok_copy = pltpu.make_async_copy(
        tok_hbm.at[:, pl.ds(pl.multiple_of(me_c * half, half), half)], tok, local_sem.at[2]
    )
    tok_copy.start()
    for h in range(heads):
        cols = slice(h * HD, (h + 1) * HD)
        pltpu.make_async_copy(q_hbm.at[:, cols], q.at[h * 128 : (h + 1) * 128], local_sem.at[0]).start()
        pltpu.make_async_copy(g_hbm.at[:, cols], g.at[h * 128 : (h + 1) * 128], local_sem.at[1]).start()
    for k in range(2):
        pltpu.make_async_copy(w_hbm.at[:, k * half : (k + 1) * half], w.at[k], local_sem.at[3]).start()
    small[0].wait()
    gath[me_x, me_z, 0] = pkv_ref[:, 0, :]
    gath[me_x, me_z, 1] = pkv_ref[:, 1, :]
    pl.semaphore_wait(barrier, len(peers) + me_h * ny)

    @pl.when(me_h == 1)
    def _():
        for o in range(ny):
            pl.semaphore_signal(ready, inc=1, device_id={"expert": far(o)}, device_id_type=MESH)


    sends = []

    def remote(src, dst, send_sem, recv_sem, peer):
        copy = pltpu.make_async_remote_copy(
            src_ref=src,
            dst_ref=dst,
            send_sem=send_sem,
            recv_sem=recv_sem,
            device_id=peer,
            device_id_type=MESH,
        )
        copy.start()
        sends.append(copy)

    z_order = sorted(range(1, nz), key=lambda o: min(o, nz - o))
    own_block = gath.at[me_x, me_z]
    for o in reversed(z_order):
        remote(own_block, own_block, zs.at[o - 1], zr.at[me_z], at_z(o))

    def forward(k, zb):
        block = gath.at[me_x, zb]
        for o in range(1, nx):
            remote(block, block, xs.at[o - 1, k], xr.at[o - 1], at_x(o))

    forward(0, me_z)

    length = len_ref[0, 0]
    lane = lax.broadcasted_iota(jnp.int32, (1, 128), 1)
    small[1].wait()
    small[2].wait()
    route_t = routes_ref[...].astype(F32)
    gate_t = gates_ref[...]
    valid = (lane < length).astype(F32)
    named, weight = [], []
    for e in range(ne):
        hit = route_t == float(e)
        named.append(jnp.max(hit.astype(F32), 0, keepdims=True))
        weight.append(jnp.sum(jnp.where(hit, gate_t, 0.0), 0, keepdims=True) * valid)
    named_all = jnp.concatenate(named, 0)
    upper = (
        lax.broadcasted_iota(jnp.int32, (128, 128), 0) <= lax.broadcasted_iota(jnp.int32, (128, 128), 1)
    ).astype(BF16)
    slot = lax.dot_general(named_all.astype(BF16), upper, NN, preferred_element_type=F32) - 1.0
    slot_id = lax.broadcasted_iota(jnp.int32, (cap, 128), 0).astype(F32)
    select, slot_gate = [], []
    for e in range(ne):
        chosen = jnp.where(slot[e : e + 1] == slot_id, named[e], 0.0)
        select.append(chosen)
        slot_gate.append(jnp.sum(chosen * weight[e], 1, keepdims=True))
    select = jnp.concatenate(select, 0).astype(BF16)
    slot_gate = jnp.concatenate(slot_gate, 0)
    tok_copy.wait()
    picked = lax.dot_general(select, tok[...], NN, preferred_element_type=F32)
    rows_out[...] = (picked * slot_gate).astype(BF16).reshape(ne, cap, half)

    def routed(there, k):
        return pltpu.make_async_remote_copy(
            src_ref=rows_out.at[there],
            dst_ref=rows_in.at[me_c, me_e],
            send_sem=es.at[k],
            recv_sem=er.at[me_e],
            device_id={"expert": there},
            device_id_type=MESH,
        )

    near_rows = [routed(at_y(o), o - 1) for o in range(1, ny)]
    far_rows = [routed(far(o), ny - 1 + o) for o in range(ny)]

    rows_in[me_c, me_e] = rows_out[me_e]

    pltpu.make_async_copy(q, q, local_sem.at[0]).wait()
    pltpu.make_async_copy(g, g, local_sem.at[1]).wait()
    row_at = lax.broadcasted_iota(jnp.int32, (128, HD), 0)
    for h in range(heads):
        part = g[h * 128 : (h + 1) * 128, :]
        g[h * 128 : (h + 1) * 128, :] = jnp.where(row_at < length, part.astype(F32), 0.0).astype(BF16)

    def forward_block(b, keys, values, causal):
        n = keys.shape[0]
        for t in range(rows_all // TILE):
            rows = slice(t * TILE, (t + 1) * TILE)
            score = lax.dot_general(keys, q[rows, :], NT, preferred_element_type=F32)
            if causal:
                key_at = lax.broadcasted_iota(jnp.int32, (n, TILE), 0)
                query_at = lax.broadcasted_iota(jnp.int32, (n, TILE), 1) % 128
                score = jnp.where(key_at <= query_at, score, -jnp.inf)
            top = jnp.max(score, 0, keepdims=True)
            exps = jnp.exp2((score - top) * SCALE2)
            probs = lax.dot_general(values, g[rows, :], NT, preferred_element_type=F32)
            stat[0, b : b + 1, rows] = top
            stat[1, b : b + 1, rows] = jnp.sum(exps, 0, keepdims=True)
            stat[2, b : b + 1, rows] = jnp.sum(exps * probs, 0, keepdims=True)
            num[b, 0:n, rows] = exps
            prob[b, 0:n, rows] = probs

    own_b = nx
    small[3].wait()
    forward_block(own_b, rkv_ref[:, 0, :], rkv_ref[:, 1, :], True)

    @pl.when(me_h == 1)
    def _():
        for copy in far_rows:
            copy.start()

    for k, o in enumerate(z_order):
        zb = (me_z + o) % nz
        block = gath.at[me_x, zb]
        pltpu.make_async_copy(block, block, zr.at[zb]).wait()
        forward(k + 1, zb)

    for copy in near_rows:
        copy.start()

    x_order = sorted(range(1, nx), key=lambda o: min(o, nx - o))
    for b, o in enumerate([0] + x_order):
        xb = (me_x + nx - o) % nx
        if o:
            came = gath.at[xb]
            pltpu.make_async_copy(came, came, xr.at[o - 1]).wait()
        forward_block(
            b, gath[xb, :, 0].reshape(blk, HD), gath[xb, :, 1].reshape(blk, HD), False
        )
        if b == 0:
            @pl.when(me_h == 0)
            def _():
                pl.semaphore_wait(ready, ny)
                for copy in far_rows:
                    copy.start()

    nb = nx + 1
    top = stat[0, 0:nb, :]
    factor = jnp.exp2((top - jnp.max(top, 0, keepdims=True)) * SCALE2)
    inverse = 1.0 / jnp.sum(stat[1, 0:nb, :] * factor, 0, keepdims=True)
    delta = jnp.sum(stat[2, 0:nb, :] * factor, 0, keepdims=True) * inverse
    stat[0, 0:nb, :] = factor * inverse
    stat[1, 0:1, :] = delta

    def backward_block(b, keys, n, at):
        for t in range(rows_all // 256):
            rows = slice(t * 256, (t + 1) * 256)
            attention = num[b, keys, rows] * stat[0, b : b + 1, rows]
            grad = attention * ((prob[b, keys, rows] - stat[1, 0:1, rows]) * SCALE)
            low_a[at, 0:n, rows] = attention.astype(BF16)
            low_g[at, 0:n, rows] = grad.astype(BF16)
        grad_v = lax.dot_general(low_a[at, 0:n, :], g[...], NN, preferred_element_type=F32)
        grad_k = lax.dot_general(low_g[at, 0:n, :], q[...], NN, preferred_element_type=F32)
        return grad_k, grad_v

    hz = nz // 2
    sub = hz * toks
    my_half, my_at = me_z // hz, me_z % hz
    halves = [1 - my_half, my_half]
    for step in range(2):
        keys = pl.ds(pl.multiple_of(halves[step] * sub, sub), sub)
        for b, o in reversed(list(enumerate([0] + x_order))):
            grad_k, grad_v = backward_block(b, keys, sub, b % 2)
            if o:
                part1[b - 1, step, 0] = grad_k.astype(BF16)
                part1[b - 1, step, 1] = grad_v.astype(BF16)
                remote(
                    part1.at[b - 1, step],
                    recv1.at[o - 1, step],
                    s1.at[o - 1, step],
                    r1.at[o - 1, step],
                    at_x(nx - o),
                )
            else:
                own_sum[step, 0] = grad_k
                own_sum[step, 1] = grad_v

    grad_k, grad_v = backward_block(own_b, slice(0, 128), 128, 1)
    own_grad[0] = grad_k
    own_grad[1] = grad_v
    own_out = pltpu.make_async_copy(own_grad, rout, local_sem.at[4])
    own_out.start()

    def swap(h, k, sources):
        for there in sources:
            came = rows_in.at[me_c, there]
            pltpu.make_async_copy(came, came, er.at[there]).wait()
        part = rows_in.at[me_c, pl.ds(pl.multiple_of(h * ny, ny), ny)]
        remote(part, part, cs.at[k], cr.at[k], sibling)

    sent = len(sends)
    swap(me_h, 0, [at_y(o) for o in range(1, ny)])

    for step in range(2):
        for o in range(1, nx):
            came = recv1.at[o - 1, step]
            pltpu.make_async_copy(came, came, r1.at[o - 1, step]).wait()
        for j in range(hz):
            keys = slice(j * toks, (j + 1) * toks)
            for kv in range(2):
                total = own_sum[step, kv, keys, :]
                for o in range(1, nx):
                    total = total + recv1[o - 1, step, kv, keys, :].astype(F32)
                own_sum[step, kv, keys, :] = total
                part2[step, j, kv] = total.astype(BF16)
        for o in range(step, hz):
            j = (my_at + o) % hz
            remote(
                part2.at[step, j],
                recv2.at[me_z],
                s2.at[step * hz + o],
                r2.at[me_z],
                {"seq": me_x * nz + halves[step] * hz + j},
            )

    for copy in sends[:sent]:
        copy.wait_send()
    swap(1 - me_h, 1, [far(o) for o in range(ny)])

    pltpu.make_async_copy(w, w, local_sem.at[3]).wait()

    def product(c):
        return lax.dot_general(
            rows_in[c].reshape(ne * cap, half), w[c], NT, preferred_element_type=F32
        )

    hidden = product(me_c)
    for k, h in enumerate([me_h, 1 - me_h]):
        other = rows_in.at[1 - me_c, pl.ds(pl.multiple_of(h * ny, ny), ny)]
        pltpu.make_async_copy(other, other, cr.at[k]).wait()
    hidden = hidden + product(1 - me_c)
    hid[...] = hidden.astype(BF16).reshape(hid.shape)
    hid_out = pltpu.make_async_copy(hid, eout, local_sem.at[5])
    hid_out.start()

    mine = pl.ds(pl.multiple_of(my_at * toks, toks), toks)
    total_k, total_v = own_sum[1, 0, mine, :], own_sum[1, 1, mine, :]
    for o in z_order:
        zb = (me_z + o) % nz
        came = recv2.at[zb]
        pltpu.make_async_copy(came, came, r2.at[zb]).wait()
        total_k = total_k + recv2[zb, 0].astype(F32)
        total_v = total_v + recv2[zb, 1].astype(F32)
    own_prompt[0] = total_k
    own_prompt[1] = total_v
    prompt_out = pltpu.make_async_copy(own_prompt, pout, local_sem.at[6])
    prompt_out.start()
    own_out.wait()
    hid_out.wait()
    prompt_out.wait()
    for copy in sends[sent:] + near_rows + far_rows:
        copy.wait_send()


def place(pin, rin, ein, pout, rout, eout):
    for kv in range(2):
        pout[:, kv, :] = pin[kv]
        rout[:, kv, :] = rin[kv]
    eout[...] = ein[...]


def local(nx, queries, out_grad, prompt_kv, resp_kv, lengths, grads, routes, gates, down_weight):
    ne = lax.axis_size("expert")
    toks = prompt_kv.shape[1]
    rows = queries.shape[2]
    width = queries.shape[3]
    heads = width // HD
    nz = lax.axis_size("seq") // nx
    features = grads.shape[3]
    half = features // 2
    hidden = down_weight.shape[1]
    cap = rows // 8
    blk = nz * toks
    vmem = pl.BlockSpec(memory_space=pltpu.VMEM)
    hbm = pl.BlockSpec(memory_space=pl.ANY)
    dma = pltpu.SemaphoreType.DMA
    out = pl.pallas_call(
        functools.partial(kernel, nx, nz),
        out_shape=[
            jax.ShapeDtypeStruct((2, toks, HD), F32),
            jax.ShapeDtypeStruct((2, rows, HD), F32),
            jax.ShapeDtypeStruct((ne, cap, hidden), BF16),
        ],
        in_specs=[pl.BlockSpec(memory_space=pltpu.SMEM)] + [hbm] * 8,
        out_specs=[hbm] * 3,
        scratch_shapes=[
            pltpu.VMEM((heads * rows, HD), BF16),
            pltpu.VMEM((heads * rows, HD), BF16),
            pltpu.VMEM((rows, half), BF16),
            pltpu.VMEM((2, hidden, half), BF16),
            pltpu.VMEM((nx, nz, 2, toks, HD), BF16),
            pltpu.VMEM((nx + 1, max(blk, rows), heads * rows), F32),
            pltpu.VMEM((nx + 1, max(blk, rows), heads * rows), F32),
            pltpu.VMEM((3, 8, heads * rows), F32),
            pltpu.VMEM((2, 128, heads * rows), BF16),
            pltpu.VMEM((2, 128, heads * rows), BF16),
            pltpu.VMEM((nx - 1, 2, 2, blk // 2, HD), BF16),
            pltpu.VMEM((nx - 1, 2, 2, blk // 2, HD), BF16),
            pltpu.VMEM((2, 2, blk // 2, HD), F32),
            pltpu.VMEM((2, nz // 2, 2, toks, HD), BF16),
            pltpu.VMEM((nz, 2, toks, HD), BF16),
            pltpu.VMEM((ne, cap, half), BF16),
            pltpu.VMEM((2, ne, cap, half), BF16),
            pltpu.VMEM((2, rows, HD), F32),
            pltpu.VMEM((2, toks, HD), F32),
            pltpu.VMEM((ne, cap, hidden), BF16),
            pltpu.VMEM((toks, 2, HD), BF16),
            pltpu.VMEM((rows, 2, HD), BF16),
            pltpu.VMEM((routes.shape[3], rows), jnp.int32),
            pltpu.VMEM((routes.shape[3], rows), F32),
            dma((11,)),
            dma((nz - 1,)),
            dma((nz,)),
            dma((nx - 1, nz)),
            dma((nx - 1,)),
            dma((ne - 1,)),
            dma((ne,)),
            dma((2,)),
            dma((2,)),
            dma((nx - 1, 2)),
            dma((nx - 1, 2)),
            dma((nz,)),
            dma((nz,)),
            pltpu.SemaphoreType.REGULAR,
        ],
        compiler_params=pltpu.CompilerParams(
            collective_id=0, has_side_effects=True, vmem_limit_bytes=60 << 20
        ),
        name="moe_attention_backward",
    )(
        lengths,
        prompt_kv[0],
        resp_kv[0, 0],
        routes[0, 0].T,
        gates[0, 0].T,
        queries[0, 0],
        out_grad[0, 0],
        grads[0, 0],
        down_weight[0],
    )
    placed = pl.pallas_call(
        place,
        out_shape=[
            jax.ShapeDtypeStruct((toks, 2, HD), F32),
            jax.ShapeDtypeStruct((rows, 2, HD), F32),
            jax.ShapeDtypeStruct((ne, cap, hidden), BF16),
        ],
        in_specs=[vmem] * 3,
        out_specs=[vmem] * 3,
        compiler_params=pltpu.CompilerParams(vmem_limit_bytes=60 << 20),
        name="place_outputs",
    )(*out)
    return (placed[0][None], placed[1][None, None], placed[2][None, :, None])


def solution(mesh):
    nx = 4 if mesh.shape["seq"] == 32 else 2
    placed = (
        P("expert", "seq", None, "mp"),
        P("expert", "seq", None, "mp"),
        P("expert", "seq", None, "mp"),
        P("expert", "seq", None, None, "mp"),
        P("expert", "seq"),
        P("expert", "seq", None, None),
        P("expert", "seq", None, None),
        P("expert", "seq", None, None),
        P("expert", "mp", None),
    )
    return jax.shard_map(
        functools.partial(local, nx),
        mesh=mesh,
        in_specs=placed,
        out_specs=(
            P("expert", "seq", None, "mp"),
            P("expert", "seq", None, None, "mp"),
            P("seq", None, "expert", None, "mp"),
        ),
        check_vma=False,
    )
```

```python
import functools
import math

import jax
import jax.numpy as jnp
from jax import lax
from jax.experimental import pallas as pl
from jax.experimental.pallas import tpu as pltpu
from jax.sharding import PartitionSpec as P

HD = 128
SCALE = HD**-0.5
SCALE2 = SCALE * math.log2(math.e)
MESH = pl.DeviceIdType.MESH
F32 = jnp.float32
BF16 = jnp.bfloat16
NT = (((1,), (1,)), ((), ()))
NN = (((1,), (0,)), ((), ()))
TILE = 512


def kernel(
    nx,
    nz,
    len_ref,
    pkv_hbm,
    rkv_hbm,
    routes_hbm,
    gates_hbm,
    q_hbm,
    g_hbm,
    tok_hbm,
    w_hbm,
    pout,
    rout,
    eout,
    q,
    g,
    tok,
    w,
    gath,
    num,
    prob,
    stat,
    low_a,
    low_g,
    part1,
    recv1,
    own_sum,
    part2,
    recv2,
    rows_out,
    rows_in,
    own_grad,
    own_prompt,
    hid,
    pkv_ref,
    rkv_ref,
    routes_ref,
    gates_ref,
    local_sem,
    zs,
    zr,
    xs,
    xr,
    es,
    er,
    cs,
    cr,
    s1,
    r1,
    s2,
    r2,
    ready,
):
    seq = lax.axis_index("seq")
    me_e = lax.axis_index("expert")
    me_c = lax.axis_index("mp")
    me_x, me_z = seq // nz, seq % nz
    ne = rows_out.shape[0]
    cap = rows_out.shape[1]
    half = rows_out.shape[2]
    rows_all = q.shape[0]
    heads = rows_all // 128
    toks = gath.shape[3]
    blk = nz * toks

    def at_x(o):
        return {"seq": (me_x + o) % nx * nz + me_z}

    def at_z(o):
        return {"seq": me_x * nz + (me_z + o) % nz}

    ny = ne // 2
    me_h, me_y = me_e // ny, me_e % ny

    def at_y(o):
        return me_h * ny + (me_y + o) % ny

    def far(o):
        return (1 - me_h) * ny + (me_y + o) % ny

    sibling = {"mp": 1 - me_c}

    barrier = pltpu.get_barrier_semaphore()
    peers = [at_x(o) for o in range(1, nx)] + [at_z(o) for o in range(1, nz)]
    peers += [{"expert": at_y(o)} for o in range(1, ny)] + [sibling]

    @pl.when(me_h == 0)
    def _():
        for o in range(ny):
            pl.semaphore_signal(barrier, inc=1, device_id={"expert": far(o)}, device_id_type=MESH)

    for peer in peers:
        pl.semaphore_signal(barrier, inc=1, device_id=peer, device_id_type=MESH)

    small = [
        pltpu.make_async_copy(src, dst, local_sem.at[7 + k])
        for k, (src, dst) in enumerate(
            [(pkv_hbm, pkv_ref), (routes_hbm, routes_ref), (gates_hbm, gates_ref), (rkv_hbm, rkv_ref)]
        )
    ]
    for copy in small:
        copy.start()
    tok_copy = pltpu.make_async_copy(
        tok_hbm.at[:, pl.ds(pl.multiple_of(me_c * half, half), half)], tok, local_sem.at[2]
    )
    tok_copy.start()
    for h in range(heads):
        cols = slice(h * HD, (h + 1) * HD)
        pltpu.make_async_copy(q_hbm.at[:, cols], q.at[h * 128 : (h + 1) * 128], local_sem.at[0]).start()
        pltpu.make_async_copy(g_hbm.at[:, cols], g.at[h * 128 : (h + 1) * 128], local_sem.at[1]).start()
    for k in range(2):
        pltpu.make_async_copy(w_hbm.at[:, k * half : (k + 1) * half], w.at[k], local_sem.at[3]).start()
    small[0].wait()
    gath[me_x, me_z, 0] = pkv_ref[:, 0, :]
    gath[me_x, me_z, 1] = pkv_ref[:, 1, :]
    pl.semaphore_wait(barrier, len(peers) + me_h * ny)

    @pl.when(me_h == 1)
    def _():
        for o in range(ny):
            pl.semaphore_signal(ready, inc=1, device_id={"expert": far(o)}, device_id_type=MESH)


    sends = []

    def remote(src, dst, send_sem, recv_sem, peer):
        copy = pltpu.make_async_remote_copy(
            src_ref=src,
            dst_ref=dst,
            send_sem=send_sem,
            recv_sem=recv_sem,
            device_id=peer,
            device_id_type=MESH,
        )
        copy.start()
        sends.append(copy)

    z_order = sorted(range(1, nz), key=lambda o: min(o, nz - o))
    own_block = gath.at[me_x, me_z]
    for o in reversed(z_order):
        remote(own_block, own_block, zs.at[o - 1], zr.at[me_z], at_z(o))

    def forward(k, zb):
        block = gath.at[me_x, zb]
        for o in range(1, nx):
            remote(block, block, xs.at[o - 1, k], xr.at[o - 1], at_x(o))

    forward(0, me_z)

    length = len_ref[0, 0]
    lane = lax.broadcasted_iota(jnp.int32, (1, 128), 1)
    small[1].wait()
    small[2].wait()
    route_t = routes_ref[...].astype(F32)
    gate_t = gates_ref[...]
    valid = (lane < length).astype(F32)
    named, weight = [], []
    for e in range(ne):
        hit = route_t == float(e)
        named.append(jnp.max(hit.astype(F32), 0, keepdims=True))
        weight.append(jnp.sum(jnp.where(hit, gate_t, 0.0), 0, keepdims=True) * valid)
    named_all = jnp.concatenate(named, 0)
    upper = (
        lax.broadcasted_iota(jnp.int32, (128, 128), 0) <= lax.broadcasted_iota(jnp.int32, (128, 128), 1)
    ).astype(BF16)
    slot = lax.dot_general(named_all.astype(BF16), upper, NN, preferred_element_type=F32) - 1.0
    slot_id = lax.broadcasted_iota(jnp.int32, (cap, 128), 0).astype(F32)
    select, slot_gate = [], []
    for e in range(ne):
        chosen = jnp.where(slot[e : e + 1] == slot_id, named[e], 0.0)
        select.append(chosen)
        slot_gate.append(jnp.sum(chosen * weight[e], 1, keepdims=True))
    select = jnp.concatenate(select, 0).astype(BF16)
    slot_gate = jnp.concatenate(slot_gate, 0)
    tok_copy.wait()
    picked = lax.dot_general(select, tok[...], NN, preferred_element_type=F32)
    rows_out[...] = (picked * slot_gate).astype(BF16).reshape(ne, cap, half)

    def routed(there, k):
        return pltpu.make_async_remote_copy(
            src_ref=rows_out.at[there],
            dst_ref=rows_in.at[me_c, me_e],
            send_sem=es.at[k],
            recv_sem=er.at[me_e],
            device_id={"expert": there},
            device_id_type=MESH,
        )

    near_rows = [routed(at_y(o), o - 1) for o in range(1, ny)]
    far_rows = [routed(far(o), ny - 1 + o) for o in range(ny)]

    rows_in[me_c, me_e] = rows_out[me_e]

    def forward_block(b, keys, values, causal):
        n = keys.shape[0]
        for t in range(rows_all // TILE):
            rows = slice(t * TILE, (t + 1) * TILE)
            score = lax.dot_general(keys, q[rows, :], NT, preferred_element_type=F32)
            if causal:
                key_at = lax.broadcasted_iota(jnp.int32, (n, TILE), 0)
                query_at = lax.broadcasted_iota(jnp.int32, (n, TILE), 1) % 128
                score = jnp.where(key_at <= query_at, score, -jnp.inf)
            top = jnp.max(score, 0, keepdims=True)
            exps = jnp.exp2((score - top) * SCALE2)
            probs = lax.dot_general(values, g[rows, :], NT, preferred_element_type=F32)
            stat[0, b : b + 1, rows] = top
            stat[1, b : b + 1, rows] = jnp.sum(exps, 0, keepdims=True)
            stat[2, b : b + 1, rows] = jnp.sum(exps * probs, 0, keepdims=True)
            num[b, 0:n, rows] = exps
            prob[b, 0:n, rows] = probs

    own_b = nx

    def own_scores():
        pltpu.make_async_copy(q, q, local_sem.at[0]).wait()
        pltpu.make_async_copy(g, g, local_sem.at[1]).wait()
        row_at = lax.broadcasted_iota(jnp.int32, (128, HD), 0)
        for h in range(heads):
            part = g[h * 128 : (h + 1) * 128, :]
            g[h * 128 : (h + 1) * 128, :] = jnp.where(row_at < length, part.astype(F32), 0.0).astype(BF16)

        small[3].wait()
        forward_block(own_b, rkv_ref[:, 0, :], rkv_ref[:, 1, :], True)

    @pl.when(me_h == 1)
    def _():
        for copy in far_rows:
            copy.start()

    for k, o in enumerate(z_order):
        zb = (me_z + o) % nz
        block = gath.at[me_x, zb]
        pltpu.make_async_copy(block, block, zr.at[zb]).wait()
        forward(k + 1, zb)
        if k == min(1, nz - 2):
            own_scores()

    for copy in near_rows:
        copy.start()

    x_order = sorted(range(1, nx), key=lambda o: min(o, nx - o))
    for b, o in enumerate([0] + x_order):
        xb = (me_x + nx - o) % nx
        if o:
            came = gath.at[xb]
            pltpu.make_async_copy(came, came, xr.at[o - 1]).wait()
        forward_block(
            b, gath[xb, :, 0].reshape(blk, HD), gath[xb, :, 1].reshape(blk, HD), False
        )
        if b == 0:
            @pl.when(me_h == 0)
            def _():
                pl.semaphore_wait(ready, ny)
                for copy in far_rows:
                    copy.start()

    nb = nx + 1
    top = stat[0, 0:nb, :]
    factor = jnp.exp2((top - jnp.max(top, 0, keepdims=True)) * SCALE2)
    inverse = 1.0 / jnp.sum(stat[1, 0:nb, :] * factor, 0, keepdims=True)
    delta = jnp.sum(stat[2, 0:nb, :] * factor, 0, keepdims=True) * inverse
    stat[0, 0:nb, :] = factor * inverse
    stat[1, 0:1, :] = delta

    def backward_block(b, keys, n, at):
        for t in range(rows_all // 256):
            rows = slice(t * 256, (t + 1) * 256)
            attention = num[b, keys, rows] * stat[0, b : b + 1, rows]
            grad = attention * ((prob[b, keys, rows] - stat[1, 0:1, rows]) * SCALE)
            low_a[at, 0:n, rows] = attention.astype(BF16)
            low_g[at, 0:n, rows] = grad.astype(BF16)
        grad_v = lax.dot_general(low_a[at, 0:n, :], g[...], NN, preferred_element_type=F32)
        grad_k = lax.dot_general(low_g[at, 0:n, :], q[...], NN, preferred_element_type=F32)
        return grad_k, grad_v

    hz = nz // 2
    sub = hz * toks
    my_half, my_at = me_z // hz, me_z % hz
    halves = [1 - my_half, my_half]
    pair = max(hz // 2, 1)
    steps = [(0, j, pair) for j in range(0, hz, pair)] + [(1, 0, hz)]
    mine = pl.ds(pl.multiple_of(my_at * toks, toks), toks)

    def produce(step):
        side, j0, nj = steps[step]
        n = nj * toks
        keys = pl.ds(pl.multiple_of(halves[side] * sub + j0 * toks, n), n)
        at = slice(j0 * toks, j0 * toks + n)
        for b, o in reversed(list(enumerate([0] + x_order))):
            grad_k, grad_v = backward_block(b, keys, n, b % 2)
            if o:
                part1[b - 1, side, 0, at, :] = grad_k.astype(BF16)
                part1[b - 1, side, 1, at, :] = grad_v.astype(BF16)
                remote(
                    part1.at[b - 1, side, :, at],
                    recv1.at[o - 1, side, :, at],
                    s1.at[o - 1, step],
                    r1.at[o - 1, step],
                    at_x(nx - o),
                )
            else:
                own_sum[side, 0, at, :] = grad_k
                own_sum[side, 1, at, :] = grad_v

    def pass_on(step):
        side, j0, nj = steps[step]
        at = slice(j0 * toks, (j0 + nj) * toks)
        for o in range(1, nx):
            came = recv1.at[o - 1, side, :, at]
            pltpu.make_async_copy(came, came, r1.at[o - 1, step]).wait()
        for j in range(j0, j0 + nj):
            keys = slice(j * toks, (j + 1) * toks)
            for kv in range(2):
                total = own_sum[side, kv, keys, :]
                for o in range(1, nx):
                    total = total + recv1[o - 1, side, kv, keys, :].astype(F32)
                own_sum[side, kv, keys, :] = total
                part2[side, j, kv] = total.astype(BF16)
        for o in range(side, nj):
            j = j0 + (my_at + o) % nj
            remote(
                part2.at[side, j],
                recv2.at[me_z],
                s2.at[side * hz + j0 + o],
                r2.at[me_z],
                {"seq": me_x * nz + halves[side] * hz + j},
            )

    def swap(h, k, sources):
        for there in sources:
            came = rows_in.at[me_c, there]
            pltpu.make_async_copy(came, came, er.at[there]).wait()
        part = rows_in.at[me_c, pl.ds(pl.multiple_of(h * ny, ny), ny)]
        remote(part, part, cs.at[k], cr.at[k], sibling)

    for step in range(len(steps) - 1):
        produce(step)
    sent = len(sends)
    grad_k, grad_v = backward_block(own_b, slice(0, 128), 128, 1)
    own_grad[0] = grad_k
    own_grad[1] = grad_v
    own_out = pltpu.make_async_copy(own_grad, rout, local_sem.at[4])
    own_out.start()
    pass_on(0)
    produce(len(steps) - 1)
    swap(me_h, 0, [at_y(o) for o in range(1, ny)])
    for step in range(1, len(steps)):
        pass_on(step)

    for copy in sends[:sent]:
        copy.wait_send()
    swap(1 - me_h, 1, [far(o) for o in range(ny)])

    pltpu.make_async_copy(w, w, local_sem.at[3]).wait()

    def product(c):
        return lax.dot_general(
            rows_in[c].reshape(ne * cap, half), w[c], NT, preferred_element_type=F32
        )

    hidden = product(me_c)
    for k, h in enumerate([me_h, 1 - me_h]):
        other = rows_in.at[1 - me_c, pl.ds(pl.multiple_of(h * ny, ny), ny)]
        pltpu.make_async_copy(other, other, cr.at[k]).wait()
    hidden = hidden + product(1 - me_c)
    hid[...] = hidden.astype(BF16).reshape(hid.shape)
    hid_out = pltpu.make_async_copy(hid, eout, local_sem.at[5])
    hid_out.start()

    mine = pl.ds(pl.multiple_of(my_at * toks, toks), toks)
    total_k, total_v = own_sum[1, 0, mine, :], own_sum[1, 1, mine, :]
    for o in z_order:
        zb = (me_z + o) % nz
        came = recv2.at[zb]
        pltpu.make_async_copy(came, came, r2.at[zb]).wait()
        total_k = total_k + recv2[zb, 0].astype(F32)
        total_v = total_v + recv2[zb, 1].astype(F32)
    own_prompt[0] = total_k
    own_prompt[1] = total_v
    prompt_out = pltpu.make_async_copy(own_prompt, pout, local_sem.at[6])
    prompt_out.start()
    own_out.wait()
    hid_out.wait()
    prompt_out.wait()
    for copy in sends[sent:] + near_rows + far_rows:
        copy.wait_send()


def place(pin, rin, ein, pout, rout, eout):
    for kv in range(2):
        pout[:, kv, :] = pin[kv]
        rout[:, kv, :] = rin[kv]
    eout[...] = ein[...]


def local(nx, queries, out_grad, prompt_kv, resp_kv, lengths, grads, routes, gates, down_weight):
    ne = lax.axis_size("expert")
    toks = prompt_kv.shape[1]
    rows = queries.shape[2]
    width = queries.shape[3]
    heads = width // HD
    nz = lax.axis_size("seq") // nx
    features = grads.shape[3]
    half = features // 2
    hidden = down_weight.shape[1]
    cap = rows // 8
    blk = nz * toks
    vmem = pl.BlockSpec(memory_space=pltpu.VMEM)
    hbm = pl.BlockSpec(memory_space=pl.ANY)
    dma = pltpu.SemaphoreType.DMA
    out = pl.pallas_call(
        functools.partial(kernel, nx, nz),
        out_shape=[
            jax.ShapeDtypeStruct((2, toks, HD), F32),
            jax.ShapeDtypeStruct((2, rows, HD), F32),
            jax.ShapeDtypeStruct((ne, cap, hidden), BF16),
        ],
        in_specs=[pl.BlockSpec(memory_space=pltpu.SMEM)] + [hbm] * 8,
        out_specs=[hbm] * 3,
        scratch_shapes=[
            pltpu.VMEM((heads * rows, HD), BF16),
            pltpu.VMEM((heads * rows, HD), BF16),
            pltpu.VMEM((rows, half), BF16),
            pltpu.VMEM((2, hidden, half), BF16),
            pltpu.VMEM((nx, nz, 2, toks, HD), BF16),
            pltpu.VMEM((nx + 1, max(blk, rows), heads * rows), F32),
            pltpu.VMEM((nx + 1, max(blk, rows), heads * rows), F32),
            pltpu.VMEM((3, 8, heads * rows), F32),
            pltpu.VMEM((2, 128, heads * rows), BF16),
            pltpu.VMEM((2, 128, heads * rows), BF16),
            pltpu.VMEM((nx - 1, 2, 2, blk // 2, HD), BF16),
            pltpu.VMEM((nx - 1, 2, 2, blk // 2, HD), BF16),
            pltpu.VMEM((2, 2, blk // 2, HD), F32),
            pltpu.VMEM((2, nz // 2, 2, toks, HD), BF16),
            pltpu.VMEM((nz, 2, toks, HD), BF16),
            pltpu.VMEM((ne, cap, half), BF16),
            pltpu.VMEM((2, ne, cap, half), BF16),
            pltpu.VMEM((2, rows, HD), F32),
            pltpu.VMEM((2, toks, HD), F32),
            pltpu.VMEM((ne, cap, hidden), BF16),
            pltpu.VMEM((toks, 2, HD), BF16),
            pltpu.VMEM((rows, 2, HD), BF16),
            pltpu.VMEM((routes.shape[3], rows), jnp.int32),
            pltpu.VMEM((routes.shape[3], rows), F32),
            dma((11,)),
            dma((nz - 1,)),
            dma((nz,)),
            dma((nx - 1, nz)),
            dma((nx - 1,)),
            dma((ne - 1,)),
            dma((ne,)),
            dma((2,)),
            dma((2,)),
            dma((nx - 1, 3)),
            dma((nx - 1, 3)),
            dma((nz,)),
            dma((nz,)),
            pltpu.SemaphoreType.REGULAR,
        ],
        compiler_params=pltpu.CompilerParams(
            collective_id=0, has_side_effects=True, vmem_limit_bytes=60 << 20
        ),
        name="moe_attention_backward",
    )(
        lengths,
        prompt_kv[0],
        resp_kv[0, 0],
        routes[0, 0].T,
        gates[0, 0].T,
        queries[0, 0],
        out_grad[0, 0],
        grads[0, 0],
        down_weight[0],
    )
    placed = pl.pallas_call(
        place,
        out_shape=[
            jax.ShapeDtypeStruct((toks, 2, HD), F32),
            jax.ShapeDtypeStruct((rows, 2, HD), F32),
            jax.ShapeDtypeStruct((ne, cap, hidden), BF16),
        ],
        in_specs=[vmem] * 3,
        out_specs=[vmem] * 3,
        compiler_params=pltpu.CompilerParams(vmem_limit_bytes=60 << 20),
        name="place_outputs",
    )(*out)
    return (placed[0][None], placed[1][None, None], placed[2][None, :, None])


def solution(mesh):
    nx = 4 if mesh.shape["seq"] == 32 else 2
    placed = (
        P("expert", "seq", None, "mp"),
        P("expert", "seq", None, "mp"),
        P("expert", "seq", None, "mp"),
        P("expert", "seq", None, None, "mp"),
        P("expert", "seq"),
        P("expert", "seq", None, None),
        P("expert", "seq", None, None),
        P("expert", "seq", None, None),
        P("expert", "mp", None),
    )
    return jax.shard_map(
        functools.partial(local, nx),
        mesh=mesh,
        in_specs=placed,
        out_specs=(
            P("expert", "seq", None, "mp"),
            P("expert", "seq", None, None, "mp"),
            P("seq", None, "expert", None, "mp"),
        ),
        check_vma=False,
    )
```

```python
import functools
import math

import jax
import jax.numpy as jnp
from jax import lax
from jax.experimental import pallas as pl
from jax.experimental.pallas import tpu as pltpu
from jax.sharding import PartitionSpec as P

HD = 128
SCALE = HD**-0.5
SCALE2 = SCALE * math.log2(math.e)
MESH = pl.DeviceIdType.MESH
F32 = jnp.float32
BF16 = jnp.bfloat16
NT = (((1,), (1,)), ((), ()))
NN = (((1,), (0,)), ((), ()))
TILE = 512


def kernel(
    nx,
    nz,
    len_ref,
    pkv_hbm,
    rkv_hbm,
    routes_hbm,
    gates_hbm,
    q_hbm,
    g_hbm,
    tok_hbm,
    w_hbm,
    pout,
    rout,
    eout,
    q,
    g,
    tok,
    w,
    gath,
    num,
    prob,
    stat,
    low_a,
    low_g,
    part1,
    recv1,
    own_sum,
    part2,
    recv2,
    rows_out,
    rows_in,
    own_grad,
    own_prompt,
    hid,
    pkv_ref,
    rkv_ref,
    routes_ref,
    gates_ref,
    local_sem,
    zs,
    zr,
    xs,
    xr,
    es,
    er,
    cs,
    cr,
    s1,
    r1,
    s2,
    r2,
    ready,
):
    seq = lax.axis_index("seq")
    me_e = lax.axis_index("expert")
    me_c = lax.axis_index("mp")
    me_x, me_z = seq // nz, seq % nz
    ne = rows_out.shape[0]
    cap = rows_out.shape[1]
    half = rows_out.shape[2]
    rows_all = q.shape[0]
    heads = rows_all // 128
    toks = gath.shape[3]
    blk = nz * toks

    def at_x(o):
        return {"seq": (me_x + o) % nx * nz + me_z}

    def at_z(o):
        return {"seq": me_x * nz + (me_z + o) % nz}

    ny = ne // 2
    me_h, me_y = me_e // ny, me_e % ny

    def at_y(o):
        return me_h * ny + (me_y + o) % ny

    def far(o):
        return (1 - me_h) * ny + (me_y + o) % ny

    sibling = {"mp": 1 - me_c}

    barrier = pltpu.get_barrier_semaphore()
    peers = [at_x(o) for o in range(1, nx)] + [at_z(o) for o in range(1, nz)]
    peers += [{"expert": at_y(o)} for o in range(1, ny)] + [sibling]

    @pl.when(me_h == 0)
    def _():
        for o in range(ny):
            pl.semaphore_signal(barrier, inc=1, device_id={"expert": far(o)}, device_id_type=MESH)

    for peer in peers:
        pl.semaphore_signal(barrier, inc=1, device_id=peer, device_id_type=MESH)

    small = [
        pltpu.make_async_copy(src, dst, local_sem.at[7 + k])
        for k, (src, dst) in enumerate(
            [(pkv_hbm, pkv_ref), (routes_hbm, routes_ref), (gates_hbm, gates_ref), (rkv_hbm, rkv_ref)]
        )
    ]
    for copy in small:
        copy.start()
    tok_copy = pltpu.make_async_copy(
        tok_hbm.at[:, pl.ds(pl.multiple_of(me_c * half, half), half)], tok, local_sem.at[2]
    )
    tok_copy.start()
    for h in range(heads):
        cols = slice(h * HD, (h + 1) * HD)
        pltpu.make_async_copy(q_hbm.at[:, cols], q.at[h * 128 : (h + 1) * 128], local_sem.at[0]).start()
        pltpu.make_async_copy(g_hbm.at[:, cols], g.at[h * 128 : (h + 1) * 128], local_sem.at[1]).start()
    for k in range(2):
        pltpu.make_async_copy(w_hbm.at[:, k * half : (k + 1) * half], w.at[k], local_sem.at[3]).start()
    small[0].wait()
    gath[me_x, me_z, 0] = pkv_ref[:, 0, :]
    gath[me_x, me_z, 1] = pkv_ref[:, 1, :]
    pl.semaphore_wait(barrier, len(peers) + me_h * ny)

    @pl.when(me_h == 1)
    def _():
        for o in range(ny):
            pl.semaphore_signal(ready, inc=1, device_id={"expert": far(o)}, device_id_type=MESH)


    sends = []

    def remote(src, dst, send_sem, recv_sem, peer):
        copy = pltpu.make_async_remote_copy(
            src_ref=src,
            dst_ref=dst,
            send_sem=send_sem,
            recv_sem=recv_sem,
            device_id=peer,
            device_id_type=MESH,
        )
        copy.start()
        sends.append(copy)

    z_order = sorted(range(1, nz), key=lambda o: min(o, nz - o))
    own_block = gath.at[me_x, me_z]
    for o in reversed(z_order):
        remote(own_block, own_block, zs.at[o - 1], zr.at[me_z], at_z(o))

    def forward(k, zb):
        block = gath.at[me_x, zb]
        for o in range(1, nx):
            remote(block, block, xs.at[o - 1, k], xr.at[o - 1], at_x(o))

    forward(0, me_z)

    length = len_ref[0, 0]
    lane = lax.broadcasted_iota(jnp.int32, (1, 128), 1)
    small[1].wait()
    small[2].wait()
    route_t = routes_ref[...].astype(F32)
    gate_t = gates_ref[...]
    valid = (lane < length).astype(F32)
    named, weight = [], []
    for e in range(ne):
        hit = route_t == float(e)
        named.append(jnp.max(hit.astype(F32), 0, keepdims=True))
        weight.append(jnp.sum(jnp.where(hit, gate_t, 0.0), 0, keepdims=True) * valid)
    named_all = jnp.concatenate(named, 0)
    upper = (
        lax.broadcasted_iota(jnp.int32, (128, 128), 0) <= lax.broadcasted_iota(jnp.int32, (128, 128), 1)
    ).astype(BF16)
    slot = lax.dot_general(named_all.astype(BF16), upper, NN, preferred_element_type=F32) - 1.0
    slot_id = lax.broadcasted_iota(jnp.int32, (cap, 128), 0).astype(F32)
    select, slot_gate = [], []
    for e in range(ne):
        chosen = jnp.where(slot[e : e + 1] == slot_id, named[e], 0.0)
        select.append(chosen)
        slot_gate.append(jnp.sum(chosen * weight[e], 1, keepdims=True))
    select = jnp.concatenate(select, 0).astype(BF16)
    slot_gate = jnp.concatenate(slot_gate, 0)
    tok_copy.wait()
    picked = lax.dot_general(select, tok[...], NN, preferred_element_type=F32)
    rows_out[...] = (picked * slot_gate).astype(BF16).reshape(ne, cap, half)

    def routed(there, k):
        return pltpu.make_async_remote_copy(
            src_ref=rows_out.at[there],
            dst_ref=rows_in.at[me_c, me_e],
            send_sem=es.at[k],
            recv_sem=er.at[me_e],
            device_id={"expert": there},
            device_id_type=MESH,
        )

    near_rows = [routed(at_y(o), o - 1) for o in range(1, ny)]
    far_rows = [routed(far(o), ny - 1 + o) for o in range(ny)]

    rows_in[me_c, me_e] = rows_out[me_e]

    pltpu.make_async_copy(q, q, local_sem.at[0]).wait()
    pltpu.make_async_copy(g, g, local_sem.at[1]).wait()
    row_at = lax.broadcasted_iota(jnp.int32, (128, HD), 0)
    for h in range(heads):
        part = g[h * 128 : (h + 1) * 128, :]
        g[h * 128 : (h + 1) * 128, :] = jnp.where(row_at < length, part.astype(F32), 0.0).astype(BF16)

    def forward_block(b, keys, values, causal):
        n = keys.shape[0]
        for t in range(rows_all // TILE):
            rows = slice(t * TILE, (t + 1) * TILE)
            score = lax.dot_general(keys, q[rows, :], NT, preferred_element_type=F32)
            if causal:
                key_at = lax.broadcasted_iota(jnp.int32, (n, TILE), 0)
                query_at = lax.broadcasted_iota(jnp.int32, (n, TILE), 1) % 128
                score = jnp.where(key_at <= query_at, score, -jnp.inf)
            top = jnp.max(score, 0, keepdims=True)
            exps = jnp.exp2((score - top) * SCALE2)
            probs = lax.dot_general(values, g[rows, :], NT, preferred_element_type=F32)
            stat[0, b : b + 1, rows] = top
            stat[1, b : b + 1, rows] = jnp.sum(exps, 0, keepdims=True)
            stat[2, b : b + 1, rows] = jnp.sum(exps * probs, 0, keepdims=True)
            num[b, 0:n, rows] = exps
            prob[b, 0:n, rows] = probs

    own_b = nx
    small[3].wait()
    forward_block(own_b, rkv_ref[:, 0, :], rkv_ref[:, 1, :], True)

    def far_start(core):
        @pl.when((me_h == 1) & (me_c == core))
        def _():
            for copy in far_rows:
                copy.start()

    far_start(0)

    for k, o in enumerate(z_order):
        zb = (me_z + o) % nz
        block = gath.at[me_x, zb]
        pltpu.make_async_copy(block, block, zr.at[zb]).wait()
        forward(k + 1, zb)
        if k == 0:
            far_start(1)

    for copy in near_rows:
        copy.start()

    x_order = sorted(range(1, nx), key=lambda o: min(o, nx - o))
    for b, o in enumerate([0] + x_order):
        xb = (me_x + nx - o) % nx
        if o:
            came = gath.at[xb]
            pltpu.make_async_copy(came, came, xr.at[o - 1]).wait()
        forward_block(
            b, gath[xb, :, 0].reshape(blk, HD), gath[xb, :, 1].reshape(blk, HD), False
        )
        if b == 0:
            @pl.when(me_h == 0)
            def _():
                pl.semaphore_wait(ready, ny)
                for copy in far_rows:
                    copy.start()

    nb = nx + 1
    top = stat[0, 0:nb, :]
    factor = jnp.exp2((top - jnp.max(top, 0, keepdims=True)) * SCALE2)
    inverse = 1.0 / jnp.sum(stat[1, 0:nb, :] * factor, 0, keepdims=True)
    delta = jnp.sum(stat[2, 0:nb, :] * factor, 0, keepdims=True) * inverse
    stat[0, 0:nb, :] = factor * inverse
    stat[1, 0:1, :] = delta

    def backward_block(b, keys, n, at):
        for t in range(rows_all // 256):
            rows = slice(t * 256, (t + 1) * 256)
            attention = num[b, keys, rows] * stat[0, b : b + 1, rows]
            grad = attention * ((prob[b, keys, rows] - stat[1, 0:1, rows]) * SCALE)
            low_a[at, 0:n, rows] = attention.astype(BF16)
            low_g[at, 0:n, rows] = grad.astype(BF16)
        grad_v = lax.dot_general(low_a[at, 0:n, :], g[...], NN, preferred_element_type=F32)
        grad_k = lax.dot_general(low_g[at, 0:n, :], q[...], NN, preferred_element_type=F32)
        return grad_k, grad_v

    hz = nz // 2
    sub = hz * toks
    my_half, my_at = me_z // hz, me_z % hz
    halves = [1 - my_half, my_half]
    for step in range(2):
        keys = pl.ds(pl.multiple_of(halves[step] * sub, sub), sub)
        for b, o in reversed(list(enumerate([0] + x_order))):
            grad_k, grad_v = backward_block(b, keys, sub, b % 2)
            if o:
                part1[b - 1, step, 0] = grad_k.astype(BF16)
                part1[b - 1, step, 1] = grad_v.astype(BF16)
                remote(
                    part1.at[b - 1, step],
                    recv1.at[o - 1, step],
                    s1.at[o - 1, step],
                    r1.at[o - 1, step],
                    at_x(nx - o),
                )
            else:
                own_sum[step, 0] = grad_k
                own_sum[step, 1] = grad_v

    grad_k, grad_v = backward_block(own_b, slice(0, 128), 128, 1)
    own_grad[0] = grad_k
    own_grad[1] = grad_v
    own_out = pltpu.make_async_copy(own_grad, rout, local_sem.at[4])
    own_out.start()

    def swap(h, k, sources):
        for there in sources:
            came = rows_in.at[me_c, there]
            pltpu.make_async_copy(came, came, er.at[there]).wait()
        part = rows_in.at[me_c, pl.ds(pl.multiple_of(h * ny, ny), ny)]
        remote(part, part, cs.at[k], cr.at[k], sibling)

    sent = len(sends)
    swap(me_h, 0, [at_y(o) for o in range(1, ny)])

    for step in range(2):
        for o in range(1, nx):
            came = recv1.at[o - 1, step]
            pltpu.make_async_copy(came, came, r1.at[o - 1, step]).wait()
        for j in range(hz):
            keys = slice(j * toks, (j + 1) * toks)
            for kv in range(2):
                total = own_sum[step, kv, keys, :]
                for o in range(1, nx):
                    total = total + recv1[o - 1, step, kv, keys, :].astype(F32)
                own_sum[step, kv, keys, :] = total
                part2[step, j, kv] = total.astype(BF16)
        for o in range(step, hz):
            j = (my_at + o) % hz
            remote(
                part2.at[step, j],
                recv2.at[me_z],
                s2.at[step * hz + o],
                r2.at[me_z],
                {"seq": me_x * nz + halves[step] * hz + j},
            )

    for copy in sends[:sent]:
        copy.wait_send()
    swap(1 - me_h, 1, [far(o) for o in range(ny)])

    pltpu.make_async_copy(w, w, local_sem.at[3]).wait()

    def product(c):
        return lax.dot_general(
            rows_in[c].reshape(ne * cap, half), w[c], NT, preferred_element_type=F32
        )

    hidden = product(me_c)
    for k, h in enumerate([me_h, 1 - me_h]):
        other = rows_in.at[1 - me_c, pl.ds(pl.multiple_of(h * ny, ny), ny)]
        pltpu.make_async_copy(other, other, cr.at[k]).wait()
    hidden = hidden + product(1 - me_c)
    hid[...] = hidden.astype(BF16).reshape(hid.shape)
    hid_out = pltpu.make_async_copy(hid, eout, local_sem.at[5])
    hid_out.start()

    mine = pl.ds(pl.multiple_of(my_at * toks, toks), toks)
    total_k, total_v = own_sum[1, 0, mine, :], own_sum[1, 1, mine, :]
    for o in z_order:
        zb = (me_z + o) % nz
        came = recv2.at[zb]
        pltpu.make_async_copy(came, came, r2.at[zb]).wait()
        total_k = total_k + recv2[zb, 0].astype(F32)
        total_v = total_v + recv2[zb, 1].astype(F32)
    own_prompt[0] = total_k
    own_prompt[1] = total_v
    prompt_out = pltpu.make_async_copy(own_prompt, pout, local_sem.at[6])
    prompt_out.start()
    own_out.wait()
    hid_out.wait()
    prompt_out.wait()
    for copy in sends[sent:] + near_rows + far_rows:
        copy.wait_send()


def place(pin, rin, ein, pout, rout, eout):
    for kv in range(2):
        pout[:, kv, :] = pin[kv]
        rout[:, kv, :] = rin[kv]
    eout[...] = ein[...]


def local(nx, queries, out_grad, prompt_kv, resp_kv, lengths, grads, routes, gates, down_weight):
    ne = lax.axis_size("expert")
    toks = prompt_kv.shape[1]
    rows = queries.shape[2]
    width = queries.shape[3]
    heads = width // HD
    nz = lax.axis_size("seq") // nx
    features = grads.shape[3]
    half = features // 2
    hidden = down_weight.shape[1]
    cap = rows // 8
    blk = nz * toks
    vmem = pl.BlockSpec(memory_space=pltpu.VMEM)
    hbm = pl.BlockSpec(memory_space=pl.ANY)
    dma = pltpu.SemaphoreType.DMA
    out = pl.pallas_call(
        functools.partial(kernel, nx, nz),
        out_shape=[
            jax.ShapeDtypeStruct((2, toks, HD), F32),
            jax.ShapeDtypeStruct((2, rows, HD), F32),
            jax.ShapeDtypeStruct((ne, cap, hidden), BF16),
        ],
        in_specs=[pl.BlockSpec(memory_space=pltpu.SMEM)] + [hbm] * 8,
        out_specs=[hbm] * 3,
        scratch_shapes=[
            pltpu.VMEM((heads * rows, HD), BF16),
            pltpu.VMEM((heads * rows, HD), BF16),
            pltpu.VMEM((rows, half), BF16),
            pltpu.VMEM((2, hidden, half), BF16),
            pltpu.VMEM((nx, nz, 2, toks, HD), BF16),
            pltpu.VMEM((nx + 1, max(blk, rows), heads * rows), F32),
            pltpu.VMEM((nx + 1, max(blk, rows), heads * rows), F32),
            pltpu.VMEM((3, 8, heads * rows), F32),
            pltpu.VMEM((2, 128, heads * rows), BF16),
            pltpu.VMEM((2, 128, heads * rows), BF16),
            pltpu.VMEM((nx - 1, 2, 2, blk // 2, HD), BF16),
            pltpu.VMEM((nx - 1, 2, 2, blk // 2, HD), BF16),
            pltpu.VMEM((2, 2, blk // 2, HD), F32),
            pltpu.VMEM((2, nz // 2, 2, toks, HD), BF16),
            pltpu.VMEM((nz, 2, toks, HD), BF16),
            pltpu.VMEM((ne, cap, half), BF16),
            pltpu.VMEM((2, ne, cap, half), BF16),
            pltpu.VMEM((2, rows, HD), F32),
            pltpu.VMEM((2, toks, HD), F32),
            pltpu.VMEM((ne, cap, hidden), BF16),
            pltpu.VMEM((toks, 2, HD), BF16),
            pltpu.VMEM((rows, 2, HD), BF16),
            pltpu.VMEM((routes.shape[3], rows), jnp.int32),
            pltpu.VMEM((routes.shape[3], rows), F32),
            dma((11,)),
            dma((nz - 1,)),
            dma((nz,)),
            dma((nx - 1, nz)),
            dma((nx - 1,)),
            dma((ne - 1,)),
            dma((ne,)),
            dma((2,)),
            dma((2,)),
            dma((nx - 1, 2)),
            dma((nx - 1, 2)),
            dma((nz,)),
            dma((nz,)),
            pltpu.SemaphoreType.REGULAR,
        ],
        compiler_params=pltpu.CompilerParams(
            collective_id=0, has_side_effects=True, vmem_limit_bytes=60 << 20
        ),
        name="moe_attention_backward",
    )(
        lengths,
        prompt_kv[0],
        resp_kv[0, 0],
        routes[0, 0].T,
        gates[0, 0].T,
        queries[0, 0],
        out_grad[0, 0],
        grads[0, 0],
        down_weight[0],
    )
    placed = pl.pallas_call(
        place,
        out_shape=[
            jax.ShapeDtypeStruct((toks, 2, HD), F32),
            jax.ShapeDtypeStruct((rows, 2, HD), F32),
            jax.ShapeDtypeStruct((ne, cap, hidden), BF16),
        ],
        in_specs=[vmem] * 3,
        out_specs=[vmem] * 3,
        compiler_params=pltpu.CompilerParams(vmem_limit_bytes=60 << 20),
        name="place_outputs",
    )(*out)
    return (placed[0][None], placed[1][None, None], placed[2][None, :, None])


def solution(mesh):
    nx = 4 if mesh.shape["seq"] == 32 else 2
    placed = (
        P("expert", "seq", None, "mp"),
        P("expert", "seq", None, "mp"),
        P("expert", "seq", None, "mp"),
        P("expert", "seq", None, None, "mp"),
        P("expert", "seq"),
        P("expert", "seq", None, None),
        P("expert", "seq", None, None),
        P("expert", "seq", None, None),
        P("expert", "mp", None),
    )
    return jax.shard_map(
        functools.partial(local, nx),
        mesh=mesh,
        in_specs=placed,
        out_specs=(
            P("expert", "seq", None, "mp"),
            P("expert", "seq", None, None, "mp"),
            P("seq", None, "expert", None, "mp"),
        ),
        check_vma=False,
    )
```
